256 devices in a mesh: ctx: 64 (over z, y_hi, x), kvh: 4 (over y_lo, core).
Axes of the slice: x: 4, y: 4 (y_hi: 2, y_lo: 2; y = y_hi * 2 + y_lo), z: 8, core: 2. Of those that a mesh axis runs over, the one named last changes fastest.
Arguments:
- hidden: bfloat16 [8192, 5120], P('ctx', 'kvh'), may hold values from -6 to 6
- w_query: bfloat16 [5120, 2560], P(None, 'kvh'), may hold values from -0.078125 to 0.078125
- query_bias: bfloat16 [2560], P('kvh'), may hold values from -5 to 5
- w_key: bfloat16 [5120, 512], P(None, 'kvh'), may hold values from -0.078125 to 0.078125
- key_bias: bfloat16 [512], P('kvh'), may hold values from -5 to 5
- w_value: bfloat16 [5120, 512], P(None, 'kvh'), may hold values from -0.078125 to 0.078125
- value_bias: bfloat16 [512], P('kvh'), may hold values from -5 to 5
- prefix_keys: bfloat16 [4, 32768, 128], P('kvh', 'ctx'), may hold values from -40 to 40
- prefix_values: bfloat16 [4, 32768, 128], P('kvh', 'ctx'), may hold values from -6 to 6
- segment: int32 [8192], P('ctx'), may hold values from 0 to 31, never falling along the last dimension, each value on 1 to 512 neighbouring positions
Outputs:
- attended: bfloat16 [8192, 2560], P('ctx', 'kvh')
- log_norm: float32 [20, 8192], P('kvh', 'ctx')
The draws below stay inside these ranges and needn't reach their ends.
Inputs may be any that keep to these rules, and one draw needn't show every extreme that they name: segment numbers never fall along the pack; each response holds 1 to 512 tokens and one holds exactly 512.
All inputs are finite; a program needn't handle non-finite values.
Results may differ from the reference program's by a relative error of at most 0.0098.
Values may be sent and summed in bfloat16 or wider, within the bound.
No kernel may reach another device: no remote copies, remote signals or barrier semaphores. Data moves between devices by JAX's collectives and lax.ppermute only.
A program may use at most 128 MiB of HBM per device.

```python
import math
import jax
import jax.numpy as jnp
import numpy as np
from jax import lax

D = 5120
HD = 128
KVH = 4
GROUP = 5
PRE_DEV = 512
RT_DEV = 128
RESP_MAX = 512
QH = 20
PREFIX = 32768
RTOK = 8192
RESP = 32
REACH = 4


def bias_direction(key):
    return 0.7 * jax.random.normal(key, (KVH, HD), jnp.float32)


def draw_query_bias(key, part):
    direction = bias_direction(key)
    key = jax.random.fold_in(key, 21)
    key_gain, key_noise = jax.random.split(key)
    gains = jnp.exp(jax.random.uniform(key_gain, (KVH, GROUP, 1), jnp.float32, -0.51, 0.34))
    noise = 0.35 * jax.random.normal(key_noise, (KVH, GROUP, HD), jnp.float32)
    return jnp.clip(direction[:, None, :] * gains + noise, -5.0, 5.0).reshape(QH * HD).astype(jnp.bfloat16)


def draw_key_bias(key, part):
    direction = bias_direction(key)
    key = jax.random.fold_in(key, 22)
    noise = 0.25 * jax.random.normal(key, (KVH, HD), jnp.float32)
    return jnp.clip(direction + noise, -5.0, 5.0).reshape(KVH * HD).astype(jnp.bfloat16)


def draw_prefix_keys(key, part):
    key = jax.random.fold_in(key, 11)
    full_shape = (KVH, PREFIX, HD)
    key_main = jax.random.fold_in(key, 0)
    base_vals = jax.random.normal(key_main, full_shape, jnp.float32)
    return jnp.clip(base_vals, -6.0, 6.0).astype(jnp.bfloat16)


def block_scale(key, dims, cuts, low, high):
    gain, own = 1.0, jax.random.fold_in(key, 6)
    for axis_at, parts in cuts:
        draws = jnp.exp(jax.random.uniform(jax.random.fold_in(own, axis_at), (parts,), jnp.float32, low / len(cuts), high / len(cuts)))
        gain = gain * jnp.repeat(draws, dims[axis_at] // parts).reshape([-1 if axis == axis_at else 1 for axis in range(len(dims))])
    return gain


def profile(amount, total, bound, slope):
    portions = [(1 << 20) // math.isqrt(rank ** slope) + 1 for rank in range(2, amount + 1)]
    spare, holding = total - bound - (amount - 1), [1] * (amount - 1)
    while spare > 0:
        movable = [i for i in range(amount - 1) if holding[i] < bound]
        whole, left = sum([portions[i] for i in movable]), spare
        for i in movable:
            addition = min(bound - holding[i], max(1, left * portions[i] // whole), spare)
            holding[i] = holding[i] + addition
            spare = spare - addition
    return np.array([bound] + holding)


def uneven_parts(stream_key, number_of, total, reach, lean):
    if number_of == 2:
        one = jax.random.randint(stream_key, (), max(1, total - reach), min(reach, total - 1) + 1)
        return jnp.stack([one, total - one])
    sizes = jnp.asarray(profile(number_of, total, reach, lean), jnp.int32)
    pairs = (number_of - 1) // 2
    source_of, taker = sizes[1:1 + 2 * pairs:2], sizes[2:2 + 2 * pairs:2]
    margin = jnp.minimum(source_of - 1, reach - taker)
    passed = jax.random.randint(jax.random.fold_in(stream_key, 1), (pairs,), 0, 1 << 20) % (margin + 1)
    sizes = sizes.at[1:1 + 2 * pairs:2].set(source_of - passed).at[2:2 + 2 * pairs:2].set(taker + passed)
    return sizes[jax.random.permutation(jax.random.fold_in(stream_key, 2), number_of)]


def gaussian(rng, extent, width, limit, cuts=(), held_as=jnp.bfloat16):
    drawn = jax.random.normal(rng, extent, jnp.float32) * width
    if len(cuts) > 0:
        drawn = block_scale(rng, extent, cuts, -0.22, 0.18) * drawn
    return jnp.clip(drawn, min=-limit, max=limit).astype(held_as)


def setup_inputs(seed: int = 0) -> dict:
    key_list = jax.random.split(jax.random.key(seed), 11)
    return {
        "hidden": gaussian(key_list[0], (RTOK, D), 1.0, 6.0, ((0, 64), (1, 4))),
        "w_query": gaussian(key_list[1], (D, QH * HD), D ** -0.5, 0.078125, ((1, 4),)),
        "query_bias": draw_query_bias(jax.random.fold_in(key_list[10], 71), 0),
        "w_key": gaussian(key_list[3], (D, KVH * HD), D ** -0.5, 0.078125, ((1, 4),)),
        "key_bias": draw_key_bias(jax.random.fold_in(key_list[10], 71), 0),
        "w_value": gaussian(key_list[5], (D, KVH * HD), D ** -0.5, 0.078125, ((1, 4),)),
        "value_bias": gaussian(key_list[6], (KVH * HD,), 1.0, 5.0, ((0, 4),)),
        "prefix_keys": draw_prefix_keys(jax.random.fold_in(key_list[10], 71), 0),
        "prefix_values": gaussian(key_list[8], (KVH, PREFIX, HD), 1.0, 6.0, ((0, 4), (1, 64))),
        "segment": jnp.searchsorted(jnp.cumsum(uneven_parts(key_list[9], RESP, RTOK, RESP_MAX, 0)), jnp.arange(RTOK), side="right").astype(jnp.int32),
    }


NEG_FILL = -1.0e30


def partial_block(queries, block_keys, block_values, allowed):
    scores = jnp.einsum("nkgd,kmd->nkgm", queries.astype(jnp.float32), block_keys.astype(jnp.float32)) * (HD ** -0.5)
    if allowed is not None:
        scores = jnp.where(allowed[:, None, None, :], scores, NEG_FILL)
    row_max = jnp.max(scores, axis=-1)
    weights = jnp.exp(scores - row_max[..., None])
    row_sum = jnp.sum(weights, axis=-1)
    rounded = lax.optimization_barrier(weights.astype(jnp.bfloat16)).astype(jnp.float32)
    mixed_out = jnp.einsum("nkgm,kmd->nkgd", rounded, block_values.astype(jnp.float32))
    return (mixed_out / row_sum[..., None]).astype(jnp.bfloat16), row_max + jnp.log(row_sum)


def absorb(running, block_out, block_norm):
    norm_max, norm_sum, weighted = running
    new_max = jnp.maximum(norm_max, block_norm)
    keep_scale = jnp.exp(norm_max - new_max)
    add_scale = jnp.exp(block_norm - new_max)
    return (new_max, norm_sum * keep_scale + add_scale,
            weighted * keep_scale[..., None] + add_scale[..., None] * block_out.astype(jnp.float32))


def project(hidden, weight, bias):
    return (jnp.dot(hidden, weight, preferred_element_type=jnp.float32) + bias.astype(jnp.float32)).astype(jnp.bfloat16)


def reference(hidden, w_query, query_bias, w_key, key_bias, w_value, value_bias, prefix_keys, prefix_values, segment):
    queries = project(hidden, w_query, query_bias).reshape(RTOK, KVH, GROUP, HD)
    new_keys = project(hidden, w_key, key_bias).reshape(RTOK, KVH, HD)
    new_values = project(hidden, w_value, value_bias).reshape(RTOK, KVH, HD)
    start_state = (jnp.full((RTOK, KVH, GROUP), NEG_FILL, jnp.float32),
                   jnp.zeros((RTOK, KVH, GROUP), jnp.float32),
                   jnp.zeros((RTOK, KVH, GROUP, HD), jnp.float32))

    def prefix_step(running, block_index):
        block_start = block_index * PRE_DEV
        block_keys = lax.dynamic_slice_in_dim(prefix_keys, block_start, PRE_DEV, 1)
        block_values = lax.dynamic_slice_in_dim(prefix_values, block_start, PRE_DEV, 1)
        block_out, block_norm = partial_block(queries, block_keys, block_values, None)
        return absorb(running, block_out, block_norm), None

    running, ignored = lax.scan(prefix_step, start_state, jnp.arange(PREFIX // PRE_DEV, dtype=jnp.int32))

    home_blocks = RTOK // RT_DEV
    block_queries = queries.reshape(home_blocks, RT_DEV, KVH, GROUP, HD)
    key_blocks = new_keys.reshape(home_blocks, RT_DEV, KVH, HD).transpose(0, 2, 1, 3)
    value_blocks = new_values.reshape(home_blocks, RT_DEV, KVH, HD).transpose(0, 2, 1, 3)
    segment_blocks = segment.reshape(home_blocks, RT_DEV)
    positions = jnp.arange(RT_DEV, dtype=jnp.int32)
    causal = positions[None, :] <= positions[:, None]
    for offset in range(REACH + 1):
        keep_count = home_blocks - offset
        shifted_keys = jnp.concatenate([jnp.zeros((offset, KVH, RT_DEV, HD), jnp.bfloat16), key_blocks[:keep_count]], 0)
        shifted_values = jnp.concatenate([jnp.zeros((offset, KVH, RT_DEV, HD), jnp.bfloat16), value_blocks[:keep_count]], 0)
        shifted_segments = jnp.concatenate([jnp.full((offset, RT_DEV), -1, jnp.int32), segment_blocks[:keep_count]], 0)
        allowed = shifted_segments[:, None, :] == segment_blocks[:, :, None]
        if offset == 0:
            allowed = allowed & causal[None]
        block_out, block_norm = jax.vmap(partial_block)(block_queries, shifted_keys, shifted_values, allowed)
        running = absorb(running, block_out.reshape(RTOK, KVH, GROUP, HD), block_norm.reshape(RTOK, KVH, GROUP))
    norm_max, norm_sum, weighted = running
    attended = (weighted / norm_sum[..., None]).astype(jnp.bfloat16).reshape(RTOK, QH * HD)
    log_norm = (norm_max + jnp.log(norm_sum)).reshape(RTOK, QH).T
    return attended, log_norm
```

```python
import functools
import math

import jax
import jax.numpy as jnp
from jax import lax
from jax.experimental import pallas as pl
from jax.experimental.pallas import tpu as pltpu
from jax.sharding import PartitionSpec as P

Z, H, X = 8, 2, 4
REACH = 4
GROUP = 5
HD = 128
TOK = 128
ROWS = GROUP * TOK
PACK = ROWS + 16
KEYS = 512
UNITS = Z
NEG_FILL = -1e30
LOG2E = math.log2(math.e)
SCALE2 = LOG2E / math.sqrt(HD)
BF16, F32 = jnp.bfloat16, jnp.float32
VMEM_LIMIT = 48 << 20


def dot_nt(a, b):
    return lax.dot_general(a, b, (((1,), (1,)), ((), ())), preferred_element_type=F32)


def dot_nn(a, b):
    return jnp.dot(a, b, preferred_element_type=F32)


def eye():
    shape = (TOK, TOK)
    return lax.broadcasted_iota(jnp.int32, shape, 0) == lax.broadcasted_iota(jnp.int32, shape, 1)


def column_to_row(column, diagonal):
    spread = jnp.where(diagonal, jnp.broadcast_to(column, (TOK, TOK)), 0.0)
    return jnp.sum(spread, axis=0, keepdims=True)


def row_to_column(row, diagonal):
    spread = jnp.where(diagonal, jnp.broadcast_to(row, (TOK, TOK)), 0.0)
    return jnp.sum(spread, axis=1, keepdims=True)


def split3(value):
    high = value.astype(BF16).astype(F32)
    rest = value - high
    middle = rest.astype(BF16).astype(F32)
    return high, middle, rest - middle


def pack_norms(norm_rows):
    parts = [split3(row) for row in norm_rows]
    rows = [part[i] for i in range(3) for part in parts]
    return jnp.concatenate(rows + [jnp.zeros((1, TOK), F32)], axis=0).astype(BF16)


def unpack_norms(packed):
    rows = packed.astype(F32)
    return rows[0:GROUP] + rows[GROUP : 2 * GROUP] + rows[2 * GROUP : 3 * GROUP]


def project_kernel(shards, first, index_ref, *refs):
    hidden_refs = refs[:shards]
    w_query_ref, w_key_ref, w_value_ref = refs[shards : shards + 3]
    rest = refs[shards + 3 :]
    step = pl.program_id(0)
    if first:
        sum_ref = rest[0]

        @pl.when(step == 0)
        def _():
            sum_ref[...] = jnp.zeros_like(sum_ref)
    else:
        before_ref, query_bias_ref, key_bias_ref, value_bias_ref, segment_ref = rest[:5]
        query_ref, packed_ref, sum_ref = rest[5:]

        @pl.when(step == 0)
        def _():
            sum_ref[...] = before_ref[...]

    for i in range(shards):

        @pl.when(step == i)
        def _():
            features = hidden_refs[i][...]
            sum_ref[:, :ROWS] += dot_nn(features, w_query_ref[...])
            sum_ref[:, ROWS : ROWS + HD] += dot_nn(features, w_key_ref[...])
            sum_ref[:, ROWS + HD :] += dot_nn(features, w_value_ref[...])

    if not first:

        @pl.when(step == shards - 1)
        def _():
            for g in range(GROUP):
                part = slice(g * HD, (g + 1) * HD)
                query_ref[g * TOK : (g + 1) * TOK, :] = (
                    sum_ref[:, part] + query_bias_ref[:, part].astype(F32)
                ).astype(BF16)
            packed_ref[0:TOK, :] = (
                sum_ref[:, ROWS : ROWS + HD] + key_bias_ref[...].astype(F32)
            ).astype(BF16)
            packed_ref[TOK : 2 * TOK, :] = (
                sum_ref[:, ROWS + HD :] + value_bias_ref[...].astype(F32)
            ).astype(BF16)
            packed_ref[2 * TOK :, :] = jnp.broadcast_to(
                segment_ref[...].astype(F32), (16, TOK)
            ).astype(BF16)


def project(index, flips, hiddens, weights, before=None, biases=None, segment=None):
    shards = len(hiddens)
    depth = hiddens[0].shape[1]
    first = before is None
    width = ROWS + 2 * HD

    def whole(shape):
        return pl.BlockSpec(shape, lambda s, index_ref: (0,) * len(shape))

    def weight_block(columns):
        def place(s, index_ref):
            flip = flips[0] + s * (flips[1] - flips[0])
            return (index_ref[0] ^ flip, 0)

        return pl.BlockSpec((depth, columns), place)

    in_specs = [whole((TOK, depth))] * shards + [weight_block(ROWS), weight_block(HD), weight_block(HD)]
    args = list(hiddens) + list(weights)
    if first:
        out_shape = jax.ShapeDtypeStruct((TOK, width), F32)
        out_specs = whole((TOK, width))
        scratch = []
    else:
        in_specs += [whole((TOK, width)), whole((1, ROWS)), whole((1, HD)), whole((1, HD)), whole((1, TOK))]
        args += [before] + list(biases) + [segment]
        out_shape = (
            jax.ShapeDtypeStruct((ROWS, HD), BF16),
            jax.ShapeDtypeStruct((2 * TOK + 16, HD), BF16),
        )
        out_specs = (whole((ROWS, HD)), whole((2 * TOK + 16, HD)))
        scratch = [pltpu.VMEM((TOK, width), F32)]
    return pl.pallas_call(
        functools.partial(project_kernel, shards, first),
        grid_spec=pltpu.PrefetchScalarGridSpec(
            num_scalar_prefetch=1,
            grid=(shards,),
            in_specs=in_specs,
            out_specs=out_specs,
            scratch_shapes=scratch,
        ),
        out_shape=out_shape,
        compiler_params=pltpu.CompilerParams(vmem_limit_bytes=VMEM_LIMIT),
        cost_estimate=pl.CostEstimate(
            flops=2_000_000_000, bytes_accessed=shards * depth * width * 2, transcendentals=0
        ),
    )(index, *args)


def prompt_kernel(count, units, block, *refs):
    query_refs = refs[:count]
    key_refs = refs[count : count + units]
    value_refs = refs[count + units : count + 2 * units]
    out_refs = refs[count + 2 * units : 2 * count + 2 * units]
    scores_ref = refs[-1]
    rows = count * ROWS
    blocks = rows // block
    groups = block // TOK
    diagonal = eye()
    norms = []

    def group_at(index):
        return index // GROUP, (index % GROUP) * TOK

    top = None
    for b in range(blocks + 1):
        high = total = mixed = None
        if b < blocks:
            parts = []
            for i in range(groups):
                which, start = group_at(b * groups + i)
                parts.append(query_refs[which][start : start + TOK, :])
            queries = jnp.concatenate(parts, axis=0)
        for j in range(units):
            columns = slice(j * KEYS, (j + 1) * KEYS)
            if b < blocks:
                scores = dot_nt(queries, key_refs[j][...])
                scores_ref[b % 2, :, columns] = scores
                for i in range(KEYS // 128):
                    tile = scores[:, i * 128 : (i + 1) * 128]
                    high = tile if high is None else jnp.maximum(high, tile)
            if b > 0:
                weights = jnp.exp2((scores_ref[(b - 1) % 2, :, columns] - top) * SCALE2)
                for i in range(KEYS // 128):
                    tile = weights[:, i * 128 : (i + 1) * 128]
                    total = tile if total is None else total + tile
                product = dot_nn(weights.astype(BF16), value_refs[j][...])
                mixed = product if mixed is None else mixed + product
        if b > 0:
            total = jnp.sum(total, axis=1, keepdims=True)
            out = (mixed / total).astype(BF16)
            norm = top * SCALE2 + jnp.log2(total)
            for i in range(groups):
                part = slice(i * TOK, (i + 1) * TOK)
                which, start = group_at((b - 1) * groups + i)
                out_refs[which][start : start + TOK, :] = out[part]
                norms.append(column_to_row(norm[part], diagonal))
        if b < blocks:
            top = jnp.max(high, axis=1, keepdims=True)
    for which in range(count):
        out_refs[which][ROWS:, :] = pack_norms(norms[which * GROUP : (which + 1) * GROUP])


def prompt_partials(queries, keys, values):
    count, units = len(queries), len(keys)
    block = 256 if (count * ROWS) % 256 == 0 else 128
    return pl.pallas_call(
        functools.partial(prompt_kernel, count, units, block),
        out_shape=[jax.ShapeDtypeStruct((PACK, HD), BF16)] * count,
        scratch_shapes=[pltpu.VMEM((2, block, units * KEYS), F32)],
        compiler_params=pltpu.CompilerParams(vmem_limit_bytes=VMEM_LIMIT),
        cost_estimate=pl.CostEstimate(
            flops=count * units * 600_000_000, bytes_accessed=units * KEYS * HD * 4, transcendentals=0
        ),
    )(*queries, *keys, *values)


def merge_kernel(parts, index_ref, query_ref, segment_ref, *refs):
    block_refs = refs[: REACH + 1]
    part_refs = refs[REACH + 1 : REACH + 1 + parts]
    attended_ref, norm_ref = refs[REACH + 1 + parts :]
    own = index_ref[0]
    diagonal = eye()
    keys = jnp.concatenate([ref[0:TOK, :] for ref in block_refs], axis=0)
    values = jnp.concatenate([ref[TOK : 2 * TOK, :] for ref in block_refs], axis=0)
    segment_row = segment_ref[...].astype(F32)
    segment = row_to_column(segment_row, diagonal)
    row_at = lax.broadcasted_iota(jnp.int32, (TOK, TOK), 0)
    column_at = lax.broadcasted_iota(jnp.int32, (TOK, TOK), 1)
    allowed = []
    for offset in range(REACH + 1):
        other = block_refs[offset][2 * TOK : 2 * TOK + 16, :].astype(F32)[0:1, :]
        same = jnp.broadcast_to(other, (TOK, TOK)) == segment
        if offset == 0:
            same = same & (column_at <= row_at)
        else:
            same = same & (jnp.broadcast_to(own, (TOK, TOK)) >= offset)
        allowed.append(same)
    allowed = jnp.concatenate(allowed, axis=1)
    part_norms = [unpack_norms(ref[ROWS:, :]) for ref in part_refs]
    fill = NEG_FILL * LOG2E
    for g in range(GROUP):
        rows = slice(g * TOK, (g + 1) * TOK)
        scores = dot_nt(query_ref[rows, :], keys) * SCALE2
        scores = jnp.where(allowed, scores, fill)
        top = jnp.max(scores, axis=1, keepdims=True)
        weights = jnp.exp2(scores - top)
        total = jnp.sum(weights, axis=1, keepdims=True)
        mixed = dot_nn(weights.astype(BF16), values)
        own_out = (mixed / total).astype(BF16)
        own_norm = column_to_row(top + jnp.log2(total), diagonal)
        norms = [norm[g : g + 1] for norm in part_norms] + [own_norm]
        outs = [ref[rows, :] for ref in part_refs] + [own_out]
        high = functools.reduce(jnp.maximum, norms)
        log_sum = high + jnp.log2(sum(jnp.exp2(norm - high) for norm in norms))
        left, right = [], []
        for norm, out in zip(norms, outs):
            share = jnp.broadcast_to(jnp.exp2(norm - log_sum), (TOK, TOK))
            share = jnp.where(diagonal, share, 0.0)
            share_high = share.astype(BF16)
            share_low = (share - share_high.astype(F32)).astype(BF16)
            left += [share_high, share_low]
            right += [out, out]
        attended = dot_nn(jnp.concatenate(left, axis=1), jnp.concatenate(right, axis=0))
        attended_ref[:, g * HD : (g + 1) * HD] = attended.astype(BF16)
        norm_ref[g : g + 1, :] = log_sum / LOG2E


def merge(index, queries, segment, blocks, parts):
    def whole(shape):
        return pl.BlockSpec(shape, lambda i, index_ref: (0,) * len(shape))

    return pl.pallas_call(
        functools.partial(merge_kernel, len(parts)),
        grid_spec=pltpu.PrefetchScalarGridSpec(
            num_scalar_prefetch=1,
            grid=(1,),
            in_specs=[whole((ROWS, HD)), whole((1, TOK))]
            + [whole((2 * TOK + 16, HD))] * len(blocks)
            + [whole((PACK, HD))] * len(parts),
            out_specs=(whole((TOK, GROUP * HD)), whole((GROUP, TOK))),
        ),
        out_shape=(
            jax.ShapeDtypeStruct((TOK, GROUP * HD), BF16),
            jax.ShapeDtypeStruct((GROUP, TOK), F32),
        ),
        compiler_params=pltpu.CompilerParams(vmem_limit_bytes=VMEM_LIMIT),
        cost_estimate=pl.CostEstimate(flops=2_000_000_000, bytes_accessed=3_000_000, transcendentals=0),
    )(index, queries, segment, *blocks, *parts)


def ctx_pairs(dz, dh, dx):
    pairs = []
    for z in range(Z):
        for h in range(H):
            for x in range(X):
                to = ((z + dz) % Z) * H * X + ((h + dh) % H) * X + (x + dx) % X
                pairs.append((z * H * X + h * X + x, to))
    return pairs


def shift(value, dz=0, dh=0, dx=0):
    return lax.ppermute(value, "ctx", ctx_pairs(dz, dh, dx))


def flip_kvh(value, bit):
    return lax.ppermute(value, "kvh", [(i, i ^ bit) for i in range(4)])


def per_device(
    hidden,
    w_query,
    query_bias,
    w_key,
    key_bias,
    w_value,
    value_bias,
    prefix_keys,
    prefix_values,
    segment,
):
    kvh_index = lax.axis_index("kvh").astype(jnp.int32).reshape(1)
    ctx_index = lax.axis_index("ctx").astype(jnp.int32).reshape(1)
    segment = segment.reshape(1, TOK)

    far = flip_kvh(hidden, 2)
    near = flip_kvh(hidden, 1)

    own_keys, own_values = prefix_keys[0], prefix_values[0]
    keys, values = [own_keys], [own_values]
    up_keys, up_values, down_keys, down_values = own_keys, own_values, own_keys, own_values
    for _ in range(Z // 2 - 1):
        up_keys, up_values = shift(up_keys, dz=1), shift(up_values, dz=1)
        down_keys, down_values = shift(down_keys, dz=-1), shift(down_values, dz=-1)
        keys += [up_keys, down_keys]
        values += [up_values, down_values]
    keys.append(shift(up_keys, dz=1))
    values.append(shift(down_values, dz=-1))

    far_near = flip_kvh(far, 1)
    weights = (w_query, w_key, w_value)
    biases = (query_bias.reshape(1, ROWS), key_bias.reshape(1, HD), value_bias.reshape(1, HD))
    sums = project(kvh_index, (0, 1), (hidden, near), weights)
    queries, packed = project(kvh_index, (2, 3), (far, far_near), weights, sums, biases, segment)

    offsets = [(dh, dx) for dh in range(H) for dx in range(X) if (dh, dx) != (0, 0)]
    peers = {(dh, dx): shift(queries, dh=dh, dx=dx) for dh, dx in offsets}
    blocks = [packed]
    count = Z * H * X
    for offset in range(1, REACH + 1):
        blocks.append(
            lax.ppermute(packed, "ctx", [(i, (i + offset) % count) for i in range(count)])
        )

    parts = []
    for call in (((1, 2), (0, 2)), ((1, 1), (1, 3)), ((1, 0), (0, 1)), ((0, 3),)):
        outs = prompt_partials([peers[offset] for offset in call], keys, values)
        for (dh, dx), out in zip(call, outs):
            parts.append(shift(out, dh=dh, dx=-dx))
    parts += prompt_partials([queries], keys, values)
    return merge(ctx_index, queries, segment, blocks, parts)


def solution(mesh):
    placed = (
        P("ctx", "kvh"),
        P(None, "kvh"),
        P("kvh"),
        P(None, "kvh"),
        P("kvh"),
        P(None, "kvh"),
        P("kvh"),
        P("kvh", "ctx", None),
        P("kvh", "ctx", None),
        P("ctx"),
    )
    return jax.shard_map(
        per_device,
        mesh=mesh,
        in_specs=placed,
        out_specs=(P("ctx", "kvh"), P("kvh", "ctx")),
        check_vma=False,
    )
```

```python
import functools
import math

import jax
import jax.numpy as jnp
from jax import lax
from jax.experimental import pallas as pl
from jax.experimental.pallas import tpu as pltpu
from jax.sharding import PartitionSpec as P

Z, H, X = 8, 2, 4
GROUP = 5
HD = 128
TOK = 128
ROWS = GROUP * TOK
PACK = ROWS + 16
BLOCK = 2 * TOK + 16
KEYS = 512
NEG_FILL = -1e30
LOG2E = math.log2(math.e)
SCALE2 = LOG2E / math.sqrt(HD)
BF16, F32 = jnp.bfloat16, jnp.float32
VMEM_LIMIT = 48 << 20


def dot_nt(a, b):
    return lax.dot_general(a, b, (((1,), (1,)), ((), ())), preferred_element_type=F32)


def dot_nn(a, b):
    return jnp.dot(a, b, preferred_element_type=F32)


def eye():
    shape = (TOK, TOK)
    return lax.broadcasted_iota(jnp.int32, shape, 0) == lax.broadcasted_iota(jnp.int32, shape, 1)


def column_to_row(column, diagonal):
    spread = jnp.where(diagonal, jnp.broadcast_to(column, (TOK, TOK)), 0.0)
    return jnp.sum(spread, axis=0, keepdims=True)


def row_to_column(row, diagonal):
    spread = jnp.where(diagonal, jnp.broadcast_to(row, (TOK, TOK)), 0.0)
    return jnp.sum(spread, axis=1, keepdims=True)


def split3(value):
    high = value.astype(BF16).astype(F32)
    rest = value - high
    middle = rest.astype(BF16).astype(F32)
    return high, middle, rest - middle


def pack_norms(norm_rows):
    parts = [split3(row) for row in norm_rows]
    rows = [part[i] for i in range(3) for part in parts]
    return jnp.concatenate(rows + [jnp.zeros((1, TOK), F32)], axis=0).astype(BF16)


def unpack_norms(packed):
    rows = packed.astype(F32)
    return rows[0:GROUP] + rows[GROUP : 2 * GROUP] + rows[2 * GROUP : 3 * GROUP]


def project_kernel(shards, first, index_ref, *refs):
    hidden_refs = refs[:shards]
    w_query_ref, w_key_ref, w_value_ref = refs[shards : shards + 3]
    rest = refs[shards + 3 :]
    step = pl.program_id(0)
    if first:
        sum_ref = rest[0]

        @pl.when(step == 0)
        def _():
            sum_ref[...] = jnp.zeros_like(sum_ref)
    else:
        before_ref, query_bias_ref, key_bias_ref, value_bias_ref, segment_ref = rest[:5]
        query_ref, sent_ref, sum_ref = rest[5:]

        @pl.when(step == 0)
        def _():
            sum_ref[...] = before_ref[...]

    for i in range(shards):

        @pl.when(step == i)
        def _():
            features = hidden_refs[i][...]
            sum_ref[:, :ROWS] += dot_nn(features, w_query_ref[...])
            sum_ref[:, ROWS : ROWS + HD] += dot_nn(features, w_key_ref[...])
            sum_ref[:, ROWS + HD :] += dot_nn(features, w_value_ref[...])

    if not first:

        @pl.when(step == shards - 1)
        def _():
            for g in range(GROUP):
                part = slice(g * HD, (g + 1) * HD)
                query = (sum_ref[:, part] + query_bias_ref[:, part].astype(F32)).astype(BF16)
                query_ref[g * TOK : (g + 1) * TOK, :] = query
                sent_ref[g * TOK : (g + 1) * TOK, :] = query
            sent_ref[ROWS : ROWS + TOK, :] = (
                sum_ref[:, ROWS : ROWS + HD] + key_bias_ref[...].astype(F32)
            ).astype(BF16)
            sent_ref[ROWS + TOK : ROWS + 2 * TOK, :] = (
                sum_ref[:, ROWS + HD :] + value_bias_ref[...].astype(F32)
            ).astype(BF16)
            sent_ref[ROWS + 2 * TOK :, :] = jnp.broadcast_to(
                segment_ref[...].astype(F32), (16, TOK)
            ).astype(BF16)


def project(index, flips, hiddens, weights, before=None, biases=None, segment=None):
    shards = len(hiddens)
    depth = hiddens[0].shape[1]
    first = before is None
    width = ROWS + 2 * HD

    def weight_block(columns):
        def place(s, index_ref):
            flip = flips[0] + s * (flips[1] - flips[0])
            return (index_ref[0] ^ flip, 0)

        return pl.BlockSpec((depth, columns), place)

    in_specs = [whole((TOK, depth))] * shards + [weight_block(ROWS), weight_block(HD), weight_block(HD)]
    args = list(hiddens) + list(weights)
    if first:
        out_shape = jax.ShapeDtypeStruct((TOK, width), F32)
        out_specs = whole((TOK, width))
        scratch = []
    else:
        in_specs += [whole((TOK, width)), whole((1, ROWS)), whole((1, HD)), whole((1, HD)), whole((1, TOK))]
        args += [before] + list(biases) + [segment]
        out_shape = (
            jax.ShapeDtypeStruct((ROWS, HD), BF16),
            jax.ShapeDtypeStruct((ROWS + BLOCK, HD), BF16),
        )
        out_specs = (whole((ROWS, HD)), whole((ROWS + BLOCK, HD)))
        scratch = [pltpu.VMEM((TOK, width), F32)]
    return pl.pallas_call(
        functools.partial(project_kernel, shards, first),
        grid_spec=pltpu.PrefetchScalarGridSpec(
            num_scalar_prefetch=1,
            grid=(shards,),
            in_specs=in_specs,
            out_specs=out_specs,
            scratch_shapes=scratch,
        ),
        out_shape=out_shape,
        compiler_params=pltpu.CompilerParams(vmem_limit_bytes=VMEM_LIMIT),
        cost_estimate=pl.CostEstimate(
            flops=2_000_000_000, bytes_accessed=shards * depth * width * 2, transcendentals=0
        ),
    )(index, *args)


def pack_kernel(keys_ref, values_ref, pack_ref):
    pack_ref[0:HD, :] = keys_ref[...].astype(F32).T.astype(BF16)
    for t in range(KEYS // HD):
        pack_ref[HD:, t * HD : (t + 1) * HD] = values_ref[t * HD : (t + 1) * HD, :]


def pack_prompt(keys, values):
    return pl.pallas_call(
        pack_kernel, out_shape=jax.ShapeDtypeStruct((2 * HD, KEYS), BF16)
    )(keys, values)


def with_ones(values):
    return jnp.concatenate([values, jnp.ones_like(values)], axis=1)


def unpack_values(unit):
    tiles = [unit[HD:, t * HD : (t + 1) * HD] for t in range(KEYS // HD)]
    return with_ones(jnp.concatenate(tiles, axis=0))


def prompt_kernel(count, early, steps, late, *refs):
    refs = list(refs)
    z_ref = refs.pop(0)
    query_refs = [refs.pop(0) for _ in range(count)]
    if late:
        before = [(refs.pop(0), refs.pop(0)) for _ in range(count)]
        all_ref = refs.pop(0)
        units = [all_ref.at[lax.rem(z_ref[0] + step, Z)] for step in steps]
        out_refs = [refs.pop(0) for _ in range(count)]
    else:
        units = [refs.pop(0) for _ in range(early)]
        after = [(refs.pop(0), refs.pop(0)) for _ in range(count)]
    scores_ref = refs.pop(0)
    groups = list(range(count * GROUP))
    blocks = [groups[i : i + 2] for i in range(0, len(groups), 2)]
    diagonal = eye()
    norms = []

    def place(group):
        start = (group % GROUP) * TOK
        return group // GROUP, slice(start, start + TOK)

    def gather(block, chosen):
        parts = [chosen[which][part, :] for which, part in map(place, block)]
        return jnp.concatenate(parts, axis=0)

    top = None
    for b in range(len(blocks) + 1):
        high = mixed = None
        if b < len(blocks):
            queries = gather(blocks[b], query_refs)
            height = len(blocks[b]) * TOK
            if late:
                high = gather(blocks[b], [ref for _, ref in before])
        if b > 0:
            done, lines = blocks[b - 1], len(blocks[b - 1]) * TOK
            if late:
                scale = jnp.exp2((gather(done, [ref for _, ref in before]) - top) * SCALE2)
                mixed = gather(done, [ref for ref, _ in before]) * jnp.concatenate([scale, scale], axis=1)
        for j, unit in enumerate(units):
            columns = slice(j * KEYS, (j + 1) * KEYS)
            if b < len(blocks):
                scores = dot_nn(queries, unit[0:HD, :])
                scores_ref[b % 2, 0:height, columns] = scores
                for i in range(KEYS // 128):
                    tile = scores[:, i * 128 : (i + 1) * 128]
                    high = tile if high is None else jnp.maximum(high, tile)
            if b > 0:
                weights = jnp.exp2((scores_ref[(b - 1) % 2, 0:lines, columns] - top) * SCALE2)
                product = dot_nn(weights.astype(BF16), unpack_values(unit[...]))
                mixed = product if mixed is None else mixed + product
        if b > 0:
            if late:
                total = mixed[:, HD:]
                out = (mixed[:, :HD] / total).astype(BF16)
                norm = top * SCALE2 + jnp.log2(total)
            for i, group in enumerate(done):
                which, part = place(group)
                lane = slice(i * TOK, (i + 1) * TOK)
                if late:
                    out_refs[which][part, :] = out[lane]
                    norms.append(jnp.sum(jnp.where(diagonal, norm[lane], 0.0), axis=0, keepdims=True))
                else:
                    after[which][0][part, :] = mixed[lane]
                    after[which][1][part, :] = jnp.broadcast_to(top[lane], (TOK, HD))
        if b < len(blocks):
            top = jnp.max(high, axis=1, keepdims=True)
    if late:
        for which in range(count):
            out_refs[which][ROWS:, :] = pack_norms(norms[which * GROUP : (which + 1) * GROUP])


def whole(shape):
    return pl.BlockSpec(shape, lambda i, index_ref: (0,) * len(shape))


STATE = (jax.ShapeDtypeStruct((ROWS, 2 * HD), F32), jax.ShapeDtypeStruct((ROWS, HD), F32))


def call_kernel(kernel, index, args, out_shape, scratch, flops):
    return pl.pallas_call(
        kernel,
        grid_spec=pltpu.PrefetchScalarGridSpec(
            num_scalar_prefetch=1,
            grid=(1,),
            in_specs=[whole(arg.shape) for arg in args],
            out_specs=[whole(out.shape) for out in out_shape],
            scratch_shapes=scratch,
        ),
        out_shape=out_shape,
        compiler_params=pltpu.CompilerParams(vmem_limit_bytes=VMEM_LIMIT),
        cost_estimate=pl.CostEstimate(
            flops=flops, bytes_accessed=sum(arg.size * arg.dtype.itemsize for arg in args), transcendentals=0
        ),
    )(index, *args)


def prompt_states(z, queries, units):
    count, early = len(queries), len(units)
    outs = call_kernel(
        functools.partial(prompt_kernel, count, early, (), False),
        z,
        list(queries) + list(units),
        list(STATE) * count,
        [pltpu.VMEM((2, 2 * TOK, early * KEYS), F32)],
        count * early * 500_000_000,
    )
    return [tuple(outs[2 * i : 2 * i + 2]) for i in range(count)]


def prompt_partials(z, queries, states, gathered, steps):
    count = len(queries)
    return call_kernel(
        functools.partial(prompt_kernel, count, 0, steps, True),
        z,
        list(queries) + [array for state in states for array in state] + [gathered],
        [jax.ShapeDtypeStruct((PACK, HD), BF16)] * count,
        [pltpu.VMEM((2, 2 * TOK, len(steps) * KEYS), F32)],
        count * len(steps) * 500_000_000,
    )


def response_kernel(index_ref, segment_ref, mixed_ref, top_ref, *refs):
    row_refs, above_ref, mixed_out_ref, top_out_ref = refs[:X], refs[X], refs[X + 1], refs[X + 2]
    own = index_ref[0]
    x = lax.rem(own, X)
    diagonal = eye()
    segment = row_to_column(segment_ref[...].astype(F32), diagonal)
    row_at = lax.broadcasted_iota(jnp.int32, (TOK, TOK), 0)
    column_at = lax.broadcasted_iota(jnp.int32, (TOK, TOK), 1)
    packs = [ref[ROWS:, :] for ref in row_refs]
    packs += [above_ref[i * BLOCK : (i + 1) * BLOCK, :] for i in range(X)]
    keys = jnp.concatenate([pack[0:TOK] for pack in packs], axis=0)
    values = with_ones(jnp.concatenate([pack[TOK : 2 * TOK] for pack in packs], axis=0))
    allowed = []
    for i, pack in enumerate(packs):
        other = pack[2 * TOK :].astype(F32)[0:1, :]
        same = jnp.broadcast_to(other, (TOK, TOK)) == segment
        x_at = jnp.broadcast_to(x, (TOK, TOK))
        if i == 0:
            same = same & (column_at <= row_at)
        elif i < X:
            same = same & (x_at >= i)
        else:
            same = same & (jnp.broadcast_to(own, (TOK, TOK)) >= X)
            if i > X:
                same = same & (x_at < i - X)
        allowed.append(same)
    allowed = jnp.concatenate(allowed, axis=1)
    for g in range(GROUP):
        rows = slice(g * TOK, (g + 1) * TOK)
        scores = jnp.where(allowed, dot_nt(row_refs[0][rows, :], keys), NEG_FILL)
        before = top_ref[rows, :]
        top = jnp.maximum(jnp.max(scores, axis=1, keepdims=True), before)
        weights = jnp.exp2((scores - top[:, 0:1]) * SCALE2)
        scale = jnp.exp2((before - top) * SCALE2)
        mixed = mixed_ref[rows, :] * jnp.concatenate([scale, scale], axis=1)
        mixed_out_ref[rows, :] = mixed + dot_nn(weights.astype(BF16), values)
        top_out_ref[rows, :] = top


def add_responses(index, segment, state, row_packs, above):
    return call_kernel(
        response_kernel,
        index,
        [segment, *state, *row_packs, above],
        list(STATE),
        [],
        1_500_000_000,
    )


def merge_kernel(parts, index_ref, *refs):
    part_refs, attended_ref, norm_ref = refs[:parts], refs[parts], refs[parts + 1]
    diagonal = eye()
    norms = [unpack_norms(ref[ROWS:, :]) for ref in part_refs]
    high = functools.reduce(jnp.maximum, norms)
    log_sum = high + jnp.log2(sum(jnp.exp2(norm - high) for norm in norms))
    norm_ref[...] = log_sum / LOG2E
    shares = [jnp.exp2(norm - log_sum) for norm in norms]
    for g in range(GROUP):
        rows = slice(g * TOK, (g + 1) * TOK)
        left, right = [], []
        for share, ref in zip(shares, part_refs):
            share = jnp.broadcast_to(share[g : g + 1], (TOK, TOK))
            share = jnp.where(diagonal, share, 0.0)
            share_high = share.astype(BF16)
            share_low = (share - share_high.astype(F32)).astype(BF16)
            out = ref[rows, :]
            left += [share_high, share_low]
            right += [out, out]
        attended = dot_nn(jnp.concatenate(left, axis=1), jnp.concatenate(right, axis=0))
        attended_ref[:, g * HD : (g + 1) * HD] = attended.astype(BF16)


def merge(index, parts):
    return call_kernel(
        functools.partial(merge_kernel, len(parts)),
        index,
        list(parts),
        [jax.ShapeDtypeStruct((TOK, GROUP * HD), BF16), jax.ShapeDtypeStruct((GROUP, TOK), F32)],
        [],
        2_000_000_000,
    )


def ctx_pairs(dz, dh, dx):
    pairs = []
    for z in range(Z):
        for h in range(H):
            for x in range(X):
                to = ((z + dz) % Z) * H * X + ((h + dh) % H) * X + (x + dx) % X
                pairs.append((z * H * X + h * X + x, to))
    return pairs


def shift(value, dz=0, dh=0, dx=0):
    return lax.ppermute(value, "ctx", ctx_pairs(dz, dh, dx))


def flip_kvh(value, bit):
    return lax.ppermute(value, "kvh", [(i, i ^ bit) for i in range(4)])


def per_device(
    hidden,
    w_query,
    query_bias,
    w_key,
    key_bias,
    w_value,
    value_bias,
    prefix_keys,
    prefix_values,
    segment,
):
    kvh_index = lax.axis_index("kvh").astype(jnp.int32).reshape(1)
    ctx_index = lax.axis_index("ctx").astype(jnp.int32).reshape(1)
    z = ctx_index // (H * X)
    segment = segment.reshape(1, TOK)

    far = flip_kvh(hidden, 2)
    near = flip_kvh(hidden, 1)

    own_unit = pack_prompt(prefix_keys[0], prefix_values[0])
    columns = [[i + H * X * k for k in range(Z)] for i in range(H * X)]
    gathered = lax.all_gather(own_unit, "ctx", axis=0, tiled=False, axis_index_groups=columns)
    early = [own_unit, shift(own_unit, dz=1), shift(own_unit, dz=-1)]
    steps = tuple(range(2, Z - 1))

    weights = (w_query, w_key, w_value)
    biases = (query_bias.reshape(1, ROWS), key_bias.reshape(1, HD), value_bias.reshape(1, HD))
    sums = project(kvh_index, (0, 1), (hidden, near), weights)
    far, sums = lax.optimization_barrier((far, sums))
    far_near = flip_kvh(far, 1)
    queries, sent = project(kvh_index, (2, 3), (far, far_near), weights, sums, biases, segment)

    row = [sent] + [shift(sent, dx=dx) for dx in range(1, X)]
    across = shift(queries, dh=1)
    peers = {(0, dx): row[dx] for dx in range(1, X)}
    peers[1, 0] = across
    for dx in (2, 1, 3):
        peers[1, dx] = shift(across, dx=dx)
    states = {}
    (states[0, 0],) = prompt_states(z, [queries], early)
    for call in (((0, 1), (0, 3)), ((0, 2), (1, 0)), ((1, 1), (1, 3), (1, 2))):
        states.update(zip(call, prompt_states(z, [peers[offset] for offset in call], early)))

    count = Z * H * X
    above = lax.ppermute(
        jnp.concatenate([sent_by[ROWS:] for sent_by in row], axis=0),
        "ctx",
        [(i, (i + X) % count) for i in range(count)],
    )
    own_state = add_responses(ctx_index, segment, states[0, 0], row, above)

    parts = []
    for call in (((1, 2), (1, 1)), ((1, 3), (0, 2)), ((1, 0), (0, 1)), ((0, 3),)):
        outs = prompt_partials(
            z, [peers[offset] for offset in call], [states[offset] for offset in call], gathered, steps
        )
        for (dh, dx), out in zip(call, outs):
            parts.append(shift(out, dh=dh, dx=-dx))
    parts += prompt_partials(z, [queries], [own_state], gathered, steps)
    return tuple(merge(ctx_index, parts))


def solution(mesh):
    placed = (
        P("ctx", "kvh"),
        P(None, "kvh"),
        P("kvh"),
        P(None, "kvh"),
        P("kvh"),
        P(None, "kvh"),
        P("kvh"),
        P("kvh", "ctx", None),
        P("kvh", "ctx", None),
        P("ctx"),
    )
    return jax.shard_map(
        per_device,
        mesh=mesh,
        in_specs=placed,
        out_specs=(P("ctx", "kvh"), P("kvh", "ctx")),
        check_vma=False,
    )
```

```python
import functools
import math

import jax
import jax.numpy as jnp
from jax import lax
from jax.experimental import pallas as pl
from jax.experimental.pallas import tpu as pltpu
from jax.sharding import PartitionSpec as P

Z, H, X = 8, 2, 4
GROUP = 5
HD = 128
TOK = 128
ROWS = GROUP * TOK
REACH = 4
PACK = ROWS + 16
BLOCK = 2 * TOK + 16
KEYS = 512
NEG_FILL = -1e30
LOG2E = math.log2(math.e)
SCALE2 = LOG2E / math.sqrt(HD)
BF16, F32 = jnp.bfloat16, jnp.float32
VMEM_LIMIT = 24 << 20
PROJECT_VMEM_LIMIT = 48 << 20


def dot_nt(a, b):
    return lax.dot_general(a, b, (((1,), (1,)), ((), ())), preferred_element_type=F32)


def dot_nn(a, b):
    return jnp.dot(a, b, preferred_element_type=F32)


def eye():
    shape = (TOK, TOK)
    return lax.broadcasted_iota(jnp.int32, shape, 0) == lax.broadcasted_iota(jnp.int32, shape, 1)


def column_to_row(column, diagonal):
    spread = jnp.where(diagonal, jnp.broadcast_to(column, (TOK, TOK)), 0.0)
    return jnp.sum(spread, axis=0, keepdims=True)


def row_to_column(row, diagonal):
    spread = jnp.where(diagonal, jnp.broadcast_to(row, (TOK, TOK)), 0.0)
    return jnp.sum(spread, axis=1, keepdims=True)


def split3(value):
    high = value.astype(BF16).astype(F32)
    rest = value - high
    middle = rest.astype(BF16).astype(F32)
    return high, middle, rest - middle


def pack_norms(norm_rows):
    parts = [split3(row) for row in norm_rows]
    rows = [part[i] for i in range(3) for part in parts]
    return jnp.concatenate(rows + [jnp.zeros((1, TOK), F32)], axis=0).astype(BF16)


def unpack_norms(packed):
    rows = packed.astype(F32)
    return rows[0:GROUP] + rows[GROUP : 2 * GROUP] + rows[2 * GROUP : 3 * GROUP]


def project_kernel(shards, first, last, index_ref, *refs):
    refs = list(refs)
    hidden_refs = [refs.pop(0) for _ in range(shards)]
    w_query_ref, w_key_ref, w_value_ref = [refs.pop(0) for _ in range(3)]
    before_ref = None if first else refs.pop(0)
    if last:
        query_bias_ref, key_bias_ref, value_bias_ref, segment_ref = [refs.pop(0) for _ in range(4)]
        query_ref, block_ref = refs.pop(0), refs.pop(0)
    sum_ref = refs.pop(0)
    step = pl.program_id(0)

    @pl.when(step == 0)
    def _():
        sum_ref[...] = jnp.zeros_like(sum_ref) if first else before_ref[...]

    for i in range(shards):

        @pl.when(step == i)
        def _():
            features = hidden_refs[i][...]
            sum_ref[:, :ROWS] += dot_nn(features, w_query_ref[...])
            sum_ref[:, ROWS : ROWS + HD] += dot_nn(features, w_key_ref[...])
            sum_ref[:, ROWS + HD :] += dot_nn(features, w_value_ref[...])

    if last:

        @pl.when(step == shards - 1)
        def _():
            for g in range(GROUP):
                part = slice(g * HD, (g + 1) * HD)
                query = (sum_ref[:, part] + query_bias_ref[:, part].astype(F32)).astype(BF16)
                query_ref[g * TOK : (g + 1) * TOK, :] = query
            block_ref[0:TOK, :] = (
                sum_ref[:, ROWS : ROWS + HD] + key_bias_ref[...].astype(F32)
            ).astype(BF16)
            block_ref[TOK : 2 * TOK, :] = (
                sum_ref[:, ROWS + HD :] + value_bias_ref[...].astype(F32)
            ).astype(BF16)
            block_ref[2 * TOK :, :] = jnp.broadcast_to(
                segment_ref[...].astype(F32), (16, TOK)
            ).astype(BF16)


def project(index, flips, hiddens, weights, before=None, biases=None, segment=None):
    shards = len(hiddens)
    depth = hiddens[0].shape[1]
    first, last = before is None, biases is not None
    width = ROWS + 2 * HD

    def weight_block(columns):
        def place(s, index_ref):
            flip = flips[0] + s * (flips[-1] - flips[0])
            return (index_ref[0] ^ flip, 0)

        return pl.BlockSpec((depth, columns), place)

    in_specs = [whole((TOK, depth))] * shards + [weight_block(ROWS), weight_block(HD), weight_block(HD)]
    args = list(hiddens) + list(weights)
    if not first:
        in_specs += [whole((TOK, width))]
        args += [before]
    if last:
        in_specs += [whole((1, ROWS)), whole((1, HD)), whole((1, HD)), whole((1, TOK))]
        args += list(biases) + [segment]
        out_shape = (
            jax.ShapeDtypeStruct((ROWS, HD), BF16),
            jax.ShapeDtypeStruct((BLOCK, HD), BF16),
        )
        out_specs = (whole((ROWS, HD)), whole((BLOCK, HD)))
        scratch = [pltpu.VMEM((TOK, width), F32)]
    else:
        out_shape = jax.ShapeDtypeStruct((TOK, width), F32)
        out_specs = whole((TOK, width))
        scratch = []
    return pl.pallas_call(
        functools.partial(project_kernel, shards, first, last),
        grid_spec=pltpu.PrefetchScalarGridSpec(
            num_scalar_prefetch=1,
            grid=(shards,),
            in_specs=in_specs,
            out_specs=out_specs,
            scratch_shapes=scratch,
        ),
        out_shape=out_shape,
        compiler_params=pltpu.CompilerParams(vmem_limit_bytes=PROJECT_VMEM_LIMIT),
        cost_estimate=pl.CostEstimate(
            flops=100_000_000, bytes_accessed=1_000_000, transcendentals=0
        ),
    )(index, *args)


def pack_kernel(keys_ref, values_ref, pack_ref):
    pack_ref[0:HD, :] = keys_ref[...].astype(F32).T.astype(BF16)
    for t in range(KEYS // HD):
        pack_ref[HD:, t * HD : (t + 1) * HD] = values_ref[t * HD : (t + 1) * HD, :]


def pack_prompt(keys, values):
    return pl.pallas_call(
        pack_kernel, out_shape=jax.ShapeDtypeStruct((2 * HD, KEYS), BF16)
    )(keys, values)


def with_ones(values):
    return jnp.concatenate([values, jnp.ones_like(values)], axis=1)


def unpack_values(unit):
    tiles = [unit[HD:, t * HD : (t + 1) * HD] for t in range(KEYS // HD)]
    return with_ones(jnp.concatenate(tiles, axis=0))


def prompt_kernel(count, unit_count, started, *refs):
    refs = list(refs[1:])
    query_refs = [refs.pop(0) for _ in range(count)]
    before = [(refs.pop(0), refs.pop(0)) for _ in range(count)] if started else []
    units = [refs.pop(0) for _ in range(unit_count)]
    out_ref, scores_ref = refs
    out_refs = [out_ref.at[i * PACK : (i + 1) * PACK] for i in range(count)]
    groups = list(range(count * GROUP))
    blocks = [groups[i : i + 2] for i in range(0, len(groups), 2)]
    diagonal = eye()
    norms = []

    def place(group):
        start = (group % GROUP) * TOK
        return group // GROUP, slice(start, start + TOK)

    def gather(block, chosen):
        parts = [chosen[which][part, :] for which, part in map(place, block)]
        return jnp.concatenate(parts, axis=0)

    top = None
    for b in range(len(blocks) + 1):
        high = mixed = None
        if b < len(blocks):
            queries = gather(blocks[b], query_refs)
            height = len(blocks[b]) * TOK
            if started:
                high = gather(blocks[b], [ref for _, ref in before])
        if b > 0:
            done, lines = blocks[b - 1], len(blocks[b - 1]) * TOK
            if started:
                scale = jnp.exp2((gather(done, [ref for _, ref in before]) - top) * SCALE2)
                mixed = gather(done, [ref for ref, _ in before]) * jnp.concatenate([scale, scale], axis=1)
        for j, unit in enumerate(units):
            columns = slice(j * KEYS, (j + 1) * KEYS)
            if b < len(blocks):
                scores = dot_nn(queries, unit[0:HD, :])
                scores_ref[b % 2, 0:height, columns] = scores
                for i in range(KEYS // 128):
                    tile = scores[:, i * 128 : (i + 1) * 128]
                    high = tile if high is None else jnp.maximum(high, tile)
            if b > 0:
                weights = jnp.exp2((scores_ref[(b - 1) % 2, 0:lines, columns] - top) * SCALE2)
                product = dot_nn(weights.astype(BF16), unpack_values(unit[...]))
                mixed = product if mixed is None else mixed + product
        if b > 0:
            total = mixed[:, HD:]
            out = (mixed[:, :HD] / total).astype(BF16)
            norm = top * SCALE2 + jnp.log2(total)
            for i, group in enumerate(done):
                which, part = place(group)
                lane = slice(i * TOK, (i + 1) * TOK)
                out_refs[which][part, :] = out[lane]
                norms.append(jnp.sum(jnp.where(diagonal, norm[lane], 0.0), axis=0, keepdims=True))
        if b < len(blocks):
            top = jnp.max(high, axis=1, keepdims=True)
    for which in range(count):
        out_refs[which][ROWS:, :] = pack_norms(norms[which * GROUP : (which + 1) * GROUP])


def whole(shape):
    return pl.BlockSpec(shape, lambda i, index_ref: (0,) * len(shape))


STATE = (jax.ShapeDtypeStruct((ROWS, 2 * HD), F32), jax.ShapeDtypeStruct((ROWS, HD), F32))


def call_kernel(kernel, index, args, out_shape, scratch, flops):
    return pl.pallas_call(
        kernel,
        grid_spec=pltpu.PrefetchScalarGridSpec(
            num_scalar_prefetch=1,
            grid=(1,),
            in_specs=[whole(arg.shape) for arg in args],
            out_specs=[whole(out.shape) for out in out_shape],
            scratch_shapes=scratch,
        ),
        out_shape=out_shape,
        compiler_params=pltpu.CompilerParams(vmem_limit_bytes=VMEM_LIMIT),
        cost_estimate=pl.CostEstimate(
            flops=flops, bytes_accessed=sum(arg.size * arg.dtype.itemsize for arg in args), transcendentals=0
        ),
    )(index, *args)


def prompt_partials(index, queries, units, states=()):
    count = len(queries)
    return call_kernel(
        functools.partial(prompt_kernel, count, len(units), bool(states)),
        index,
        list(queries) + [array for state in states for array in state] + list(units),
        [jax.ShapeDtypeStruct((count * PACK, HD), BF16)],
        [pltpu.VMEM((2, 2 * TOK, len(units) * KEYS), F32)],
        count * len(units) * 450_000_000,
    )[0]


def response_kernel(index_ref, segment_ref, query_ref, *refs):
    block_refs, (mixed_out_ref, top_out_ref) = refs[: REACH + 1], refs[REACH + 1 :]
    own = index_ref[0]
    diagonal = eye()
    segment = row_to_column(segment_ref[...].astype(F32), diagonal)
    row_at = lax.broadcasted_iota(jnp.int32, (TOK, TOK), 0)
    column_at = lax.broadcasted_iota(jnp.int32, (TOK, TOK), 1)
    keys = jnp.concatenate([ref[0:TOK, :] for ref in block_refs], axis=0)
    values = with_ones(jnp.concatenate([ref[TOK : 2 * TOK, :] for ref in block_refs], axis=0))
    allowed = []
    for offset, ref in enumerate(block_refs):
        other = ref[2 * TOK :, :].astype(F32)[0:1, :]
        same = jnp.broadcast_to(other, (TOK, TOK)) == segment
        if offset == 0:
            same = same & (column_at <= row_at)
        else:
            same = same & (jnp.broadcast_to(own, (TOK, TOK)) >= offset)
        allowed.append(same)
    allowed = jnp.concatenate(allowed, axis=1)
    for g in range(GROUP):
        rows = slice(g * TOK, (g + 1) * TOK)
        scores = jnp.where(allowed, dot_nt(query_ref[rows, :], keys), NEG_FILL)
        top = jnp.max(scores, axis=1, keepdims=True)
        weights = jnp.exp2((scores - top) * SCALE2)
        mixed_out_ref[rows, :] = dot_nn(weights.astype(BF16), values)
        top_out_ref[rows, :] = jnp.broadcast_to(top, (TOK, HD))


def response_state(index, segment, queries, blocks):
    return call_kernel(
        response_kernel, index, [segment, queries, *blocks], list(STATE), [], 1_200_000_000
    )


def log_sum_of(norms):
    high = functools.reduce(jnp.maximum, norms)
    return high + jnp.log2(sum(jnp.exp2(norm - high) for norm in norms))


def weighted(shares, outs, diagonal):
    left, right = [], []
    for share, out in zip(shares, outs):
        share = jnp.where(diagonal, jnp.broadcast_to(share, (TOK, TOK)), 0.0)
        share_high = share.astype(BF16)
        share_low = (share - share_high.astype(F32)).astype(BF16)
        left += [share_high, share_low]
        right += [out, out]
    return dot_nn(jnp.concatenate(left, axis=1), jnp.concatenate(right, axis=0))


def pair_kernel(index_ref, mine_ref, first_ref, second_ref, *out_refs):
    diagonal = eye()
    others = ((first_ref, 0), (first_ref, PACK), (second_ref, 0))
    for i, other in enumerate(others):
        sources = ((mine_ref, i * PACK), other)
        norms = [unpack_norms(ref[start + ROWS : start + PACK, :]) for ref, start in sources]
        log_sum = log_sum_of(norms)
        shares = [jnp.exp2(norm - log_sum) for norm in norms]
        for g in range(GROUP):
            outs = [ref[start + g * TOK : start + (g + 1) * TOK, :] for ref, start in sources]
            mixed = weighted([share[g : g + 1] for share in shares], outs, diagonal)
            out_refs[i][g * TOK : (g + 1) * TOK, :] = mixed.astype(BF16)
        out_refs[i][ROWS:, :] = pack_norms([log_sum[g : g + 1] for g in range(GROUP)])


def merge_pairs(index, mine, first, second):
    return call_kernel(
        pair_kernel,
        index,
        [mine, first, second],
        [jax.ShapeDtypeStruct((PACK, HD), BF16)] * (X - 1),
        [],
        1_500_000_000,
    )


def merge_kernel(parts, index_ref, *refs):
    part_refs, attended_ref, norm_ref = refs[:parts], refs[parts], refs[parts + 1]
    part_refs = [ref.at[ref.shape[0] - PACK : ref.shape[0]] for ref in part_refs]
    diagonal = eye()
    norms = [unpack_norms(ref[ROWS:PACK, :]) for ref in part_refs]
    log_sum = log_sum_of(norms)
    norm_ref[...] = log_sum / LOG2E
    shares = [jnp.exp2(norm - log_sum) for norm in norms]
    for g in range(GROUP):
        outs = [ref[g * TOK : (g + 1) * TOK, :] for ref in part_refs]
        attended = weighted([share[g : g + 1] for share in shares], outs, diagonal)
        attended_ref[:, g * HD : (g + 1) * HD] = attended.astype(BF16)


def merge(index, parts):
    return call_kernel(
        functools.partial(merge_kernel, len(parts)),
        index,
        list(parts),
        [jax.ShapeDtypeStruct((TOK, GROUP * HD), BF16), jax.ShapeDtypeStruct((GROUP, TOK), F32)],
        [],
        1_500_000_000,
    )


def ctx_pairs(dz, dh, dx):
    pairs = []
    for z in range(Z):
        for h in range(H):
            for x in range(X):
                to = ((z + dz) % Z) * H * X + ((h + dh) % H) * X + (x + dx) % X
                pairs.append((z * H * X + h * X + x, to))
    return pairs


def shift(value, dz=0, dh=0, dx=0):
    return lax.ppermute(value, "ctx", ctx_pairs(dz, dh, dx))


def flip_kvh(value, bit):
    return lax.ppermute(value, "kvh", [(i, i ^ bit) for i in range(4)])


def per_device(
    hidden,
    w_query,
    query_bias,
    w_key,
    key_bias,
    w_value,
    value_bias,
    prefix_keys,
    prefix_values,
    segment,
):
    kvh_index = lax.axis_index("kvh").astype(jnp.int32).reshape(1)
    ctx_index = lax.axis_index("ctx").astype(jnp.int32).reshape(1)
    segment = segment.reshape(1, TOK)

    barrier = lax.optimization_barrier
    far = flip_kvh(hidden, 2)
    near = flip_kvh(hidden, 1)

    own_unit = pack_prompt(prefix_keys[0], prefix_values[0])
    near, own_unit = barrier((near, own_unit))
    up1, down1 = shift(own_unit, dz=1), shift(own_unit, dz=-1)

    weights = (w_query, w_key, w_value)
    biases = (query_bias.reshape(1, ROWS), key_bias.reshape(1, HD), value_bias.reshape(1, HD))
    sums = project(kvh_index, (0, 1), (hidden, near), weights)
    far, sums, up1, down1 = barrier((far, sums, up1, down1))
    far_near = flip_kvh(far, 1)
    up2, down2 = shift(up1, dz=1), shift(down1, dz=-1)
    queries, block = project(kvh_index, (2, 3), (far, far_near), weights, sums, biases, segment)

    across = shift(queries, dh=1)
    row1 = shift(queries, dx=1)
    up2, down2, queries_again = barrier((up2, down2, queries))
    up3, down3 = shift(up2, dz=1), shift(down2, dz=-1)
    row3, row2 = shift(queries_again, dx=3), shift(queries_again, dx=2)
    up4 = shift(up3, dz=1)
    beyond1, beyond3 = shift(across, dx=1), shift(across, dx=3)
    beyond2 = shift(row2, dh=1)
    units = [own_unit, up1, down1, up2, down2, up3, down3, up4]

    first = prompt_partials(ctx_index, [beyond1, beyond3], units)
    first, block = barrier((first, block))
    first = shift(first, dh=1)
    second = shift(prompt_partials(ctx_index, [beyond2, across], units), dh=1)
    mine = prompt_partials(ctx_index, [row1, row3, row2], units)

    count = Z * H * X

    def behind(value, offset):
        return lax.ppermute(value, "ctx", [(i, (i + offset) % count) for i in range(count)])

    block1 = behind(block, 1)
    pair = behind(jnp.concatenate([block, block1], axis=0), 2)
    blocks = [block, block1, pair[:BLOCK], pair[BLOCK:], behind(block, 4)]
    state = response_state(ctx_index, segment, queries, blocks)

    pairs = merge_pairs(ctx_index, mine, first, second)
    parts = [shift(part, dx=-dx) for dx, part in zip((1, 3, 2), pairs)]
    queries, pairs = barrier((queries, pairs))
    own = prompt_partials(ctx_index, [queries], units, [state])
    return tuple(merge(ctx_index, [own, second] + parts))


def solution(mesh):
    placed = (
        P("ctx", "kvh"),
        P(None, "kvh"),
        P("kvh"),
        P(None, "kvh"),
        P("kvh"),
        P(None, "kvh"),
        P("kvh"),
        P("kvh", "ctx", None),
        P("kvh", "ctx", None),
        P("ctx"),
    )
    return jax.shard_map(
        per_device,
        mesh=mesh,
        in_specs=placed,
        out_specs=(P("ctx", "kvh"), P("kvh", "ctx")),
        check_vma=False,
    )
```

```python
import functools
import math

import jax
import jax.numpy as jnp
from jax import lax
from jax.experimental import pallas as pl
from jax.experimental.pallas import tpu as pltpu
from jax.sharding import PartitionSpec as P

Z, H, X = 8, 2, 4
GROUP = 5
HD = 128
TOK = 128
ROWS = GROUP * TOK
REACH = 4
SLICES = 5
PACK = ROWS + 16
BLOCK = 2 * TOK + 16
KEYS = 512
NEG_FILL = -1e30
LOG2E = math.log2(math.e)
SCALE2 = LOG2E / math.sqrt(HD)
BF16, F32 = jnp.bfloat16, jnp.float32
VMEM_LIMIT = 24 << 20
PROJECT_VMEM_LIMIT = 48 << 20


def dot_nt(a, b):
    return lax.dot_general(a, b, (((1,), (1,)), ((), ())), preferred_element_type=F32)


def dot_nn(a, b):
    return jnp.dot(a, b, preferred_element_type=F32)


def eye():
    shape = (TOK, TOK)
    return lax.broadcasted_iota(jnp.int32, shape, 0) == lax.broadcasted_iota(jnp.int32, shape, 1)


def column_to_row(column, diagonal):
    spread = jnp.where(diagonal, jnp.broadcast_to(column, (TOK, TOK)), 0.0)
    return jnp.sum(spread, axis=0, keepdims=True)


def row_to_column(row, diagonal):
    spread = jnp.where(diagonal, jnp.broadcast_to(row, (TOK, TOK)), 0.0)
    return jnp.sum(spread, axis=1, keepdims=True)


def split3(value):
    high = value.astype(BF16).astype(F32)
    rest = value - high
    middle = rest.astype(BF16).astype(F32)
    return high, middle, rest - middle


def pack_norms(norm_rows):
    parts = [split3(row) for row in norm_rows]
    rows = [part[i] for i in range(3) for part in parts]
    return jnp.concatenate(rows + [jnp.zeros((1, TOK), F32)], axis=0).astype(BF16)


def unpack_norms(packed):
    rows = packed.astype(F32)
    return rows[0:GROUP] + rows[GROUP : 2 * GROUP] + rows[2 * GROUP : 3 * GROUP]


def project_kernel(shards, first, last, index_ref, *refs):
    refs = list(refs)
    hidden_refs = [refs.pop(0) for _ in range(shards)]
    w_query_refs = [refs.pop(0) for _ in range(SLICES)]
    w_key_ref, w_value_ref = refs.pop(0), refs.pop(0)
    before_ref = None if first else refs.pop(0)
    if last:
        query_bias_ref, key_bias_ref, value_bias_ref, segment_ref = [refs.pop(0) for _ in range(4)]
        query_ref, block_ref = refs.pop(0), refs.pop(0)
    sum_ref = refs.pop(0)
    step = pl.program_id(0)

    @pl.when(step == 0)
    def _():
        sum_ref[...] = jnp.zeros_like(sum_ref) if first else before_ref[...]

    for i in range(shards):

        @pl.when(step == i)
        def _():
            features = hidden_refs[i][...]
            depth = features.shape[1] // SLICES
            sum_ref[:, :ROWS] += sum(
                dot_nn(features[:, k * depth : (k + 1) * depth], ref[...])
                for k, ref in enumerate(w_query_refs)
            )
            sum_ref[:, ROWS : ROWS + HD] += dot_nn(features, w_key_ref[...])
            sum_ref[:, ROWS + HD :] += dot_nn(features, w_value_ref[...])

    if last:

        @pl.when(step == shards - 1)
        def _():
            for g in range(GROUP):
                part = slice(g * HD, (g + 1) * HD)
                query = (sum_ref[:, part] + query_bias_ref[:, part].astype(F32)).astype(BF16)
                query_ref[g * TOK : (g + 1) * TOK, :] = query
            numbers = jnp.broadcast_to(segment_ref[...].astype(F32), (16, TOK)).astype(BF16)
            query_ref[ROWS:, :] = numbers
            block_ref[0:TOK, :] = (
                sum_ref[:, ROWS : ROWS + HD] + key_bias_ref[...].astype(F32)
            ).astype(BF16)
            block_ref[TOK : 2 * TOK, :] = (
                sum_ref[:, ROWS + HD :] + value_bias_ref[...].astype(F32)
            ).astype(BF16)
            block_ref[2 * TOK :, :] = numbers


def project(index, flips, hiddens, weights, before=None, biases=None, segment=None):
    shards = len(hiddens)
    depth = hiddens[0].shape[1]
    first, last = before is None, biases is not None
    width = ROWS + 2 * HD

    def weight_block(columns, parts=1, part=0):
        def place(s, index_ref):
            flip = flips[0] + s * (flips[-1] - flips[0])
            return ((index_ref[0] ^ flip) * parts + part, 0)

        return pl.BlockSpec((depth // parts, columns), place)

    in_specs = [whole((TOK, depth))] * shards
    in_specs += [weight_block(ROWS, SLICES, part) for part in range(SLICES)]
    in_specs += [weight_block(HD), weight_block(HD)]
    args = list(hiddens) + [weights[0]] * SLICES + list(weights[1:])
    if not first:
        in_specs += [whole((TOK, width))]
        args += [before]
    if last:
        in_specs += [whole((1, ROWS)), whole((1, HD)), whole((1, HD)), whole((1, TOK))]
        args += list(biases) + [segment]
        out_shape = (
            jax.ShapeDtypeStruct((PACK, HD), BF16),
            jax.ShapeDtypeStruct((BLOCK, HD), BF16),
        )
        out_specs = (whole((PACK, HD)), whole((BLOCK, HD)))
        scratch = [pltpu.VMEM((TOK, width), F32)]
    else:
        out_shape = jax.ShapeDtypeStruct((TOK, width), F32)
        out_specs = whole((TOK, width))
        scratch = []
    return pl.pallas_call(
        functools.partial(project_kernel, shards, first, last),
        grid_spec=pltpu.PrefetchScalarGridSpec(
            num_scalar_prefetch=1,
            grid=(shards,),
            in_specs=in_specs,
            out_specs=out_specs,
            scratch_shapes=scratch,
        ),
        out_shape=out_shape,
        compiler_params=pltpu.CompilerParams(vmem_limit_bytes=PROJECT_VMEM_LIMIT),
        cost_estimate=pl.CostEstimate(
            flops=100_000_000, bytes_accessed=1_000_000, transcendentals=0
        ),
    )(index, *args)


def pack_kernel(keys_ref, values_ref, pack_ref):
    pack_ref[0:HD, :] = keys_ref[...].astype(F32).T.astype(BF16)
    for t in range(KEYS // HD):
        pack_ref[HD:, t * HD : (t + 1) * HD] = values_ref[t * HD : (t + 1) * HD, :]


def pack_prompt(keys, values):
    return pl.pallas_call(
        pack_kernel, out_shape=jax.ShapeDtypeStruct((2 * HD, KEYS), BF16)
    )(keys, values)


def with_ones(values):
    return jnp.concatenate([values, jnp.ones_like(values)], axis=1)


def unpack_values(unit):
    tiles = [unit[HD:, t * HD : (t + 1) * HD] for t in range(KEYS // HD)]
    return with_ones(jnp.concatenate(tiles, axis=0))


def allowed_keys(index_ref, query_ref, offset, block_refs, diagonal):
    own = index_ref[0]
    h, x = lax.rem(own // X, H), lax.rem(own, X)
    home = own + X * (lax.rem(h + offset[0], H) - h) + lax.rem(x + X - offset[1], X) - x
    numbers = row_to_column(query_ref[ROWS:, :].astype(F32)[0:1, :], diagonal)
    row_at = lax.broadcasted_iota(jnp.int32, (TOK, TOK), 0)
    column_at = lax.broadcasted_iota(jnp.int32, (TOK, TOK), 1)
    masks = []
    for ref, back in zip(block_refs, (0, H * X)):
        other = ref[2 * TOK :, :].astype(F32)[0:1, :]
        same = jnp.broadcast_to(other, (TOK, TOK)) == numbers
        ahead = jnp.broadcast_to(home - own + back, (TOK, TOK))
        same = same & (ahead >= 0) & (ahead <= REACH) & ((ahead > 0) | (column_at <= row_at))
        masks.append(same & (jnp.broadcast_to(own, (TOK, TOK)) >= back))
    return jnp.concatenate(masks, axis=1)


def prompt_kernel(offsets, unit_count, index_ref, *refs):
    refs = list(refs)
    count = len(offsets)
    query_refs = [refs.pop(0) for _ in range(count)]
    units = [refs.pop(0) for _ in range(unit_count)]
    block_refs = [refs.pop(0), refs.pop(0)]
    out_ref, scores_ref = refs
    out_refs = [out_ref.at[i * PACK : (i + 1) * PACK] for i in range(count)]
    groups = list(range(count * GROUP))
    blocks = [groups[i : i + 2] for i in range(0, len(groups), 2)]
    diagonal = eye()
    norms = []
    masks = [
        allowed_keys(index_ref, ref, offset, block_refs, diagonal)
        for ref, offset in zip(query_refs, offsets)
    ]
    block_keys = jnp.concatenate([ref[0:TOK, :] for ref in block_refs], axis=0)
    block_values = with_ones(jnp.concatenate([ref[TOK : 2 * TOK, :] for ref in block_refs], axis=0))

    def place(group):
        start = (group % GROUP) * TOK
        return group // GROUP, slice(start, start + TOK)

    top = None
    for b in range(len(blocks) + 1):
        high = mixed = None
        if b < len(blocks):
            parts = [query_refs[which][part, :] for which, part in map(place, blocks[b])]
            queries = jnp.concatenate(parts, axis=0)
            mask = jnp.concatenate([masks[group // GROUP] for group in blocks[b]], axis=0)
            height = len(blocks[b]) * TOK
        if b > 0:
            done, lines = blocks[b - 1], len(blocks[b - 1]) * TOK
        for j in range(unit_count + 1):
            response = j == unit_count
            width = 2 * TOK if response else KEYS
            columns = slice(j * KEYS, j * KEYS + width)
            if b < len(blocks):
                if response:
                    scores = jnp.where(mask, dot_nt(queries, block_keys), NEG_FILL)
                else:
                    scores = dot_nn(queries, units[j][0:HD, :])
                scores_ref[b % 2, 0:height, columns] = scores
                for i in range(width // 128):
                    tile = scores[:, i * 128 : (i + 1) * 128]
                    high = tile if high is None else jnp.maximum(high, tile)
            if b > 0:
                weights = jnp.exp2((scores_ref[(b - 1) % 2, 0:lines, columns] - top) * SCALE2)
                values = block_values if response else unpack_values(units[j][...])
                product = dot_nn(weights.astype(BF16), values)
                mixed = product if mixed is None else mixed + product
        if b > 0:
            total = mixed[:, HD:]
            out = (mixed[:, :HD] / total).astype(BF16)
            norm = top * SCALE2 + jnp.log2(total)
            for i, group in enumerate(done):
                which, part = place(group)
                lane = slice(i * TOK, (i + 1) * TOK)
                out_refs[which][part, :] = out[lane]
                norms.append(jnp.sum(jnp.where(diagonal, norm[lane], 0.0), axis=0, keepdims=True))
        if b < len(blocks):
            top = jnp.max(high, axis=1, keepdims=True)
    for which in range(count):
        out_refs[which][ROWS:, :] = pack_norms(norms[which * GROUP : (which + 1) * GROUP])


def whole(shape):
    return pl.BlockSpec(shape, lambda i, index_ref: (0,) * len(shape))


def call_kernel(kernel, index, args, out_shape, scratch, flops):
    return pl.pallas_call(
        kernel,
        grid_spec=pltpu.PrefetchScalarGridSpec(
            num_scalar_prefetch=1,
            grid=(1,),
            in_specs=[whole(arg.shape) for arg in args],
            out_specs=[whole(out.shape) for out in out_shape],
            scratch_shapes=scratch,
        ),
        out_shape=out_shape,
        compiler_params=pltpu.CompilerParams(vmem_limit_bytes=VMEM_LIMIT),
        cost_estimate=pl.CostEstimate(
            flops=flops, bytes_accessed=sum(arg.size * arg.dtype.itemsize for arg in args), transcendentals=0
        ),
    )(index, *args)


def prompt_partials(index, queries, offsets, units, blocks):
    count = len(queries)
    return call_kernel(
        functools.partial(prompt_kernel, offsets, len(units)),
        index,
        list(queries) + list(units) + list(blocks),
        [jax.ShapeDtypeStruct((count * PACK, HD), BF16)],
        [pltpu.VMEM((2, 2 * TOK, len(units) * KEYS + 2 * TOK), F32)],
        count * len(units) * 450_000_000,
    )[0]


def log_sum_of(norms):
    high = functools.reduce(jnp.maximum, norms)
    return high + jnp.log2(sum(jnp.exp2(norm - high) for norm in norms))


def weighted(shares, outs, diagonal):
    left, right = [], []
    for share, out in zip(shares, outs):
        share = jnp.where(diagonal, jnp.broadcast_to(share, (TOK, TOK)), 0.0)
        share_high = share.astype(BF16)
        share_low = (share - share_high.astype(F32)).astype(BF16)
        left += [share_high, share_low]
        right += [out, out]
    return dot_nn(jnp.concatenate(left, axis=1), jnp.concatenate(right, axis=0))


def pair_kernel(index_ref, mine_ref, first_ref, second_ref, *out_refs):
    diagonal = eye()
    others = ((first_ref, 0), (first_ref, PACK), (second_ref, 0))
    for i, other in enumerate(others):
        sources = ((mine_ref, i * PACK), other)
        norms = [unpack_norms(ref[start + ROWS : start + PACK, :]) for ref, start in sources]
        log_sum = log_sum_of(norms)
        shares = [jnp.exp2(norm - log_sum) for norm in norms]
        for g in range(GROUP):
            outs = [ref[start + g * TOK : start + (g + 1) * TOK, :] for ref, start in sources]
            mixed = weighted([share[g : g + 1] for share in shares], outs, diagonal)
            out_refs[i][g * TOK : (g + 1) * TOK, :] = mixed.astype(BF16)
        out_refs[i][ROWS:, :] = pack_norms([log_sum[g : g + 1] for g in range(GROUP)])


def merge_pairs(index, mine, first, second):
    return call_kernel(
        pair_kernel,
        index,
        [mine, first, second],
        [jax.ShapeDtypeStruct((PACK, HD), BF16)] * (X - 1),
        [],
        1_500_000_000,
    )


def merge_kernel(parts, index_ref, *refs):
    part_refs, attended_ref, norm_ref = refs[:parts], refs[parts], refs[parts + 1]
    part_refs = [ref.at[ref.shape[0] - PACK : ref.shape[0]] for ref in part_refs]
    diagonal = eye()
    norms = [unpack_norms(ref[ROWS:PACK, :]) for ref in part_refs]
    log_sum = log_sum_of(norms)
    norm_ref[...] = log_sum / LOG2E
    shares = [jnp.exp2(norm - log_sum) for norm in norms]
    for g in range(GROUP):
        outs = [ref[g * TOK : (g + 1) * TOK, :] for ref in part_refs]
        attended = weighted([share[g : g + 1] for share in shares], outs, diagonal)
        attended_ref[:, g * HD : (g + 1) * HD] = attended.astype(BF16)


def merge(index, parts):
    return call_kernel(
        functools.partial(merge_kernel, len(parts)),
        index,
        list(parts),
        [jax.ShapeDtypeStruct((TOK, GROUP * HD), BF16), jax.ShapeDtypeStruct((GROUP, TOK), F32)],
        [],
        1_500_000_000,
    )


def ctx_pairs(dz, dh, dx):
    pairs = []
    for z in range(Z):
        for h in range(H):
            for x in range(X):
                to = ((z + dz) % Z) * H * X + ((h + dh) % H) * X + (x + dx) % X
                pairs.append((z * H * X + h * X + x, to))
    return pairs


def shift(value, dz=0, dh=0, dx=0):
    return lax.ppermute(value, "ctx", ctx_pairs(dz, dh, dx))


def flip_kvh(value, bit):
    return lax.ppermute(value, "kvh", [(i, i ^ bit) for i in range(4)])


def per_device(
    hidden,
    w_query,
    query_bias,
    w_key,
    key_bias,
    w_value,
    value_bias,
    prefix_keys,
    prefix_values,
    segment,
):
    kvh_index = lax.axis_index("kvh").astype(jnp.int32).reshape(1)
    ctx_index = lax.axis_index("ctx").astype(jnp.int32).reshape(1)
    segment = segment.reshape(1, TOK)

    barrier = lax.optimization_barrier
    far = flip_kvh(hidden, 2)
    near = flip_kvh(hidden, 1)

    own_unit = pack_prompt(prefix_keys[0], prefix_values[0])
    near, own_unit = barrier((near, own_unit))
    up1, down1 = shift(own_unit, dz=1), shift(own_unit, dz=-1)

    weights = (w_query, w_key, w_value)
    biases = (query_bias.reshape(1, ROWS), key_bias.reshape(1, HD), value_bias.reshape(1, HD))
    sums = project(kvh_index, (0, 1), (hidden, near), weights)
    far, sums, up1, down1 = barrier((far, sums, up1, down1))
    far_near = flip_kvh(far, 1)
    up2, down2 = shift(up1, dz=1), shift(down1, dz=-1)
    queries, block = project(kvh_index, (2, 3), (far, far_near), weights, sums, biases, segment)

    across = shift(queries, dh=1)
    row1, row3 = shift(queries, dx=1), shift(queries, dx=3)
    block8 = shift(block, dz=1)
    up2, down2, row1, row3, block8 = barrier((up2, down2, row1, row3, block8))
    up3, down3 = shift(up2, dz=1), shift(down2, dz=-1)
    row2 = shift(queries, dx=2)
    up4 = shift(up3, dz=1)
    beyond1, beyond3 = shift(across, dx=1), shift(across, dx=3)
    beyond2 = shift(row2, dh=1)
    units = [own_unit, up1, down1, up2, down2, up3, down3, up4]
    blocks = [block, block8]

    def partials(*pairs):
        offsets, chosen = zip(*pairs)
        return prompt_partials(ctx_index, chosen, offsets, units, blocks)

    first = shift(partials(((1, 1), beyond1), ((1, 3), beyond3)), dh=1)
    second = shift(partials(((1, 2), beyond2), ((1, 0), across)), dh=1)
    mine = partials(((0, 1), row1), ((0, 3), row3), ((0, 2), row2))
    homeward = merge_pairs(ctx_index, mine, first, second)
    parts = [shift(part, dx=-dx) for dx, part in zip((1, 3, 2), homeward)]
    queries, homeward = barrier((queries, homeward))
    own = partials(((0, 0), queries))
    return tuple(merge(ctx_index, [own, second] + parts))


def solution(mesh):
    placed = (
        P("ctx", "kvh"),
        P(None, "kvh"),
        P("kvh"),
        P(None, "kvh"),
        P("kvh"),
        P(None, "kvh"),
        P("kvh"),
        P("kvh", "ctx", None),
        P("kvh", "ctx", None),
        P("ctx"),
    )
    return jax.shard_map(
        per_device,
        mesh=mesh,
        in_specs=placed,
        out_specs=(P("ctx", "kvh"), P("kvh", "ctx")),
        check_vma=False,
    )
```

```python
import functools
import math

import jax
import jax.numpy as jnp
from jax import lax
from jax.experimental import pallas as pl
from jax.experimental.pallas import tpu as pltpu
from jax.sharding import PartitionSpec as P

Z, H, X = 8, 2, 4
GROUP = 5
HD = 128
TOK = 128
ROWS = GROUP * TOK
REACH = 4
SLICES = 5
PACK = ROWS + 16
BLOCK = 2 * TOK + 16
KEYS = 512
NEG_FILL = -1e30
LOG2E = math.log2(math.e)
SCALE2 = LOG2E / math.sqrt(HD)
BF16, F32 = jnp.bfloat16, jnp.float32
VMEM_LIMIT = 24 << 20
PROJECT_VMEM_LIMIT = 48 << 20


def dot_nt(a, b):
    return lax.dot_general(a, b, (((1,), (1,)), ((), ())), preferred_element_type=F32)


def dot_nn(a, b):
    return jnp.dot(a, b, preferred_element_type=F32)


def eye():
    shape = (TOK, TOK)
    return lax.broadcasted_iota(jnp.int32, shape, 0) == lax.broadcasted_iota(jnp.int32, shape, 1)


def column_to_row(column, diagonal):
    spread = jnp.where(diagonal, jnp.broadcast_to(column, (TOK, TOK)), 0.0)
    return jnp.sum(spread, axis=0, keepdims=True)


def row_to_column(row, diagonal):
    spread = jnp.where(diagonal, jnp.broadcast_to(row, (TOK, TOK)), 0.0)
    return jnp.sum(spread, axis=1, keepdims=True)


def split3(value):
    high = value.astype(BF16).astype(F32)
    rest = value - high
    middle = rest.astype(BF16).astype(F32)
    return high, middle, rest - middle


def pack_norms(norm_rows):
    parts = [split3(row) for row in norm_rows]
    rows = [part[i] for i in range(3) for part in parts]
    return jnp.concatenate(rows + [jnp.zeros((1, TOK), F32)], axis=0).astype(BF16)


def unpack_norms(packed):
    rows = packed.astype(F32)
    return rows[0:GROUP] + rows[GROUP : 2 * GROUP] + rows[2 * GROUP : 3 * GROUP]


def project_kernel(shards, first, last, index_ref, *refs):
    refs = list(refs)
    hidden_refs = [refs.pop(0) for _ in range(shards)]
    w_query_refs = [refs.pop(0) for _ in range(SLICES)]
    w_key_ref, w_value_ref = refs.pop(0), refs.pop(0)
    before_ref = None if first else refs.pop(0)
    if last:
        query_bias_ref, key_bias_ref, value_bias_ref, segment_ref = [refs.pop(0) for _ in range(4)]
        query_ref, block_ref = refs.pop(0), refs.pop(0)
    sum_ref = refs.pop(0)
    step = pl.program_id(0)

    @pl.when(step == 0)
    def _():
        sum_ref[...] = jnp.zeros_like(sum_ref) if first else before_ref[...]

    for i in range(shards):

        @pl.when(step == i)
        def _():
            features = hidden_refs[i][...]
            depth = features.shape[1] // SLICES
            sum_ref[:, :ROWS] += sum(
                dot_nn(features[:, k * depth : (k + 1) * depth], ref[...])
                for k, ref in enumerate(w_query_refs)
            )
            sum_ref[:, ROWS : ROWS + HD] += dot_nn(features, w_key_ref[...])
            sum_ref[:, ROWS + HD :] += dot_nn(features, w_value_ref[...])

    if last:

        @pl.when(step == shards - 1)
        def _():
            for g in range(GROUP):
                part = slice(g * HD, (g + 1) * HD)
                query = (sum_ref[:, part] + query_bias_ref[:, part].astype(F32)).astype(BF16)
                query_ref[g * TOK : (g + 1) * TOK, :] = query
            numbers = jnp.broadcast_to(segment_ref[...].astype(F32), (16, TOK)).astype(BF16)
            query_ref[ROWS:, :] = numbers
            block_ref[0:TOK, :] = (
                sum_ref[:, ROWS : ROWS + HD] + key_bias_ref[...].astype(F32)
            ).astype(BF16)
            block_ref[TOK : 2 * TOK, :] = (
                sum_ref[:, ROWS + HD :] + value_bias_ref[...].astype(F32)
            ).astype(BF16)
            block_ref[2 * TOK :, :] = numbers


def project(index, flips, hiddens, weights, before=None, biases=None, segment=None):
    shards = len(hiddens)
    depth = hiddens[0].shape[1]
    first, last = before is None, biases is not None
    width = ROWS + 2 * HD

    def weight_block(columns, parts=1, part=0):
        def place(s, index_ref):
            flip = flips[0] + s * (flips[-1] - flips[0])
            return ((index_ref[0] ^ flip) * parts + part, 0)

        return pl.BlockSpec((depth // parts, columns), place)

    in_specs = [whole((TOK, depth))] * shards
    in_specs += [weight_block(ROWS, SLICES, part) for part in range(SLICES)]
    in_specs += [weight_block(HD), weight_block(HD)]
    args = list(hiddens) + [weights[0]] * SLICES + list(weights[1:])
    if not first:
        in_specs += [whole((TOK, width))]
        args += [before]
    if last:
        in_specs += [whole((1, ROWS)), whole((1, HD)), whole((1, HD)), whole((1, TOK))]
        args += list(biases) + [segment]
        out_shape = (
            jax.ShapeDtypeStruct((PACK, HD), BF16),
            jax.ShapeDtypeStruct((BLOCK, HD), BF16),
        )
        out_specs = (whole((PACK, HD)), whole((BLOCK, HD)))
        scratch = [pltpu.VMEM((TOK, width), F32)]
    else:
        out_shape = jax.ShapeDtypeStruct((TOK, width), F32)
        out_specs = whole((TOK, width))
        scratch = []
    return pl.pallas_call(
        functools.partial(project_kernel, shards, first, last),
        grid_spec=pltpu.PrefetchScalarGridSpec(
            num_scalar_prefetch=1,
            grid=(shards,),
            in_specs=in_specs,
            out_specs=out_specs,
            scratch_shapes=scratch,
        ),
        out_shape=out_shape,
        compiler_params=pltpu.CompilerParams(vmem_limit_bytes=PROJECT_VMEM_LIMIT),
        cost_estimate=pl.CostEstimate(
            flops=100_000_000, bytes_accessed=1_000_000, transcendentals=0
        ),
    )(index, *args)


def pack_kernel(keys_ref, values_ref, pack_ref):
    pack_ref[0:HD, :] = keys_ref[...].astype(F32).T.astype(BF16)
    for t in range(KEYS // HD):
        pack_ref[HD:, t * HD : (t + 1) * HD] = values_ref[t * HD : (t + 1) * HD, :]


def pack_prompt(keys, values):
    return pl.pallas_call(
        pack_kernel, out_shape=jax.ShapeDtypeStruct((2 * HD, KEYS), BF16)
    )(keys, values)


def with_ones(values):
    return jnp.concatenate([values, jnp.ones_like(values)], axis=1)


def unpack_values(unit):
    tiles = [unit[HD:, t * HD : (t + 1) * HD] for t in range(KEYS // HD)]
    return with_ones(jnp.concatenate(tiles, axis=0))


def allowed_keys(index_ref, query_ref, offset, block_refs, diagonal):
    own = index_ref[0]
    h, x = lax.rem(own // X, H), lax.rem(own, X)
    home = own + X * (lax.rem(h + offset[0], H) - h) + lax.rem(x + X - offset[1], X) - x
    numbers = row_to_column(query_ref[ROWS:, :].astype(F32)[0:1, :], diagonal)
    row_at = lax.broadcasted_iota(jnp.int32, (TOK, TOK), 0)
    column_at = lax.broadcasted_iota(jnp.int32, (TOK, TOK), 1)
    masks = []
    for ref, back in zip(block_refs, (0, H * X)):
        other = ref[2 * TOK :, :].astype(F32)[0:1, :]
        same = jnp.broadcast_to(other, (TOK, TOK)) == numbers
        ahead = jnp.broadcast_to(home - own + back, (TOK, TOK))
        same = same & (ahead >= 0) & (ahead <= REACH) & ((ahead > 0) | (column_at <= row_at))
        masks.append(same & (jnp.broadcast_to(own, (TOK, TOK)) >= back))
    return jnp.concatenate(masks, axis=1)


def prompt_kernel(offsets, unit_count, index_ref, *refs):
    refs = list(refs)
    count = len(offsets)
    query_refs = [refs.pop(0) for _ in range(count)]
    units = [refs.pop(0) for _ in range(unit_count)]
    block_refs = [refs.pop(0), refs.pop(0)]
    out_ref, scores_ref = refs
    out_refs = [out_ref.at[i * PACK : (i + 1) * PACK] for i in range(count)]
    groups = list(range(count * GROUP))
    blocks = [groups[i : i + 2] for i in range(0, len(groups), 2)]
    diagonal = eye()
    norms = []
    masks = [
        allowed_keys(index_ref, ref, offset, block_refs, diagonal)
        for ref, offset in zip(query_refs, offsets)
    ]
    block_keys = jnp.concatenate([ref[0:TOK, :] for ref in block_refs], axis=0)
    block_values = with_ones(jnp.concatenate([ref[TOK : 2 * TOK, :] for ref in block_refs], axis=0))

    def place(group):
        start = (group % GROUP) * TOK
        return group // GROUP, slice(start, start + TOK)

    top = None
    for b in range(len(blocks) + 1):
        high = mixed = None
        if b < len(blocks):
            parts = [query_refs[which][part, :] for which, part in map(place, blocks[b])]
            queries = jnp.concatenate(parts, axis=0)
            mask = jnp.concatenate([masks[group // GROUP] for group in blocks[b]], axis=0)
            height = len(blocks[b]) * TOK
        if b > 0:
            done, lines = blocks[b - 1], len(blocks[b - 1]) * TOK
        for j in range(unit_count + 1):
            response = j == unit_count
            width = 2 * TOK if response else KEYS
            columns = slice(j * KEYS, j * KEYS + width)
            if b < len(blocks):
                if response:
                    scores = jnp.where(mask, dot_nt(queries, block_keys), NEG_FILL)
                else:
                    scores = dot_nn(queries, units[j][0:HD, :])
                scores_ref[b % 2, 0:height, columns] = scores
                for i in range(width // 128):
                    tile = scores[:, i * 128 : (i + 1) * 128]
                    high = tile if high is None else jnp.maximum(high, tile)
            if b > 0:
                weights = jnp.exp2((scores_ref[(b - 1) % 2, 0:lines, columns] - top) * SCALE2)
                values = block_values if response else unpack_values(units[j][...])
                product = dot_nn(weights.astype(BF16), values)
                mixed = product if mixed is None else mixed + product
        if b > 0:
            total = mixed[:, HD:]
            out = (mixed[:, :HD] / total).astype(BF16)
            norm = top * SCALE2 + jnp.log2(total)
            for i, group in enumerate(done):
                which, part = place(group)
                lane = slice(i * TOK, (i + 1) * TOK)
                out_refs[which][part, :] = out[lane]
                norms.append(jnp.sum(jnp.where(diagonal, norm[lane], 0.0), axis=0, keepdims=True))
        if b < len(blocks):
            top = jnp.max(high, axis=1, keepdims=True)
    for which in range(count):
        out_refs[which][ROWS:, :] = pack_norms(norms[which * GROUP : (which + 1) * GROUP])


def whole(shape):
    return pl.BlockSpec(shape, lambda i, index_ref: (0,) * len(shape))


def call_kernel(kernel, index, args, out_shape, scratch, flops):
    return pl.pallas_call(
        kernel,
        grid_spec=pltpu.PrefetchScalarGridSpec(
            num_scalar_prefetch=1,
            grid=(1,),
            in_specs=[whole(arg.shape) for arg in args],
            out_specs=[whole(out.shape) for out in out_shape],
            scratch_shapes=scratch,
        ),
        out_shape=out_shape,
        compiler_params=pltpu.CompilerParams(vmem_limit_bytes=VMEM_LIMIT),
        cost_estimate=pl.CostEstimate(
            flops=flops, bytes_accessed=sum(arg.size * arg.dtype.itemsize for arg in args), transcendentals=0
        ),
    )(index, *args)


def prompt_partials(index, queries, offsets, units, blocks):
    count = len(queries)
    return call_kernel(
        functools.partial(prompt_kernel, offsets, len(units)),
        index,
        list(queries) + list(units) + list(blocks),
        [jax.ShapeDtypeStruct((count * PACK, HD), BF16)],
        [pltpu.VMEM((2, 2 * TOK, len(units) * KEYS + 2 * TOK), F32)],
        count * len(units) * 450_000_000,
    )[0]


def log_sum_of(norms):
    high = functools.reduce(jnp.maximum, norms)
    return high + jnp.log2(sum(jnp.exp2(norm - high) for norm in norms))


def weighted(shares, outs, diagonal):
    left, right = [], []
    for share, out in zip(shares, outs):
        share = jnp.where(diagonal, jnp.broadcast_to(share, (TOK, TOK)), 0.0)
        share_high = share.astype(BF16)
        share_low = (share - share_high.astype(F32)).astype(BF16)
        left += [share_high, share_low]
        right += [out, out]
    return dot_nn(jnp.concatenate(left, axis=1), jnp.concatenate(right, axis=0))


def pair_kernel(index_ref, mine_ref, first_ref, second_ref, *out_refs):
    diagonal = eye()
    others = ((first_ref, 0), (first_ref, PACK), (second_ref, 0))
    for i, other in enumerate(others):
        sources = ((mine_ref, i * PACK), other)
        norms = [unpack_norms(ref[start + ROWS : start + PACK, :]) for ref, start in sources]
        log_sum = log_sum_of(norms)
        shares = [jnp.exp2(norm - log_sum) for norm in norms]
        for g in range(GROUP):
            outs = [ref[start + g * TOK : start + (g + 1) * TOK, :] for ref, start in sources]
            mixed = weighted([share[g : g + 1] for share in shares], outs, diagonal)
            out_refs[i][g * TOK : (g + 1) * TOK, :] = mixed.astype(BF16)
        out_refs[i][ROWS:, :] = pack_norms([log_sum[g : g + 1] for g in range(GROUP)])


def merge_pairs(index, mine, first, second):
    return call_kernel(
        pair_kernel,
        index,
        [mine, first, second],
        [jax.ShapeDtypeStruct((PACK, HD), BF16)] * (X - 1),
        [],
        1_500_000_000,
    )


def merge_kernel(parts, index_ref, *refs):
    part_refs, attended_ref, norm_ref = refs[:parts], refs[parts], refs[parts + 1]
    part_refs = [ref.at[ref.shape[0] - PACK : ref.shape[0]] for ref in part_refs]
    diagonal = eye()
    norms = [unpack_norms(ref[ROWS:PACK, :]) for ref in part_refs]
    log_sum = log_sum_of(norms)
    norm_ref[...] = log_sum / LOG2E
    shares = [jnp.exp2(norm - log_sum) for norm in norms]
    for g in range(GROUP):
        outs = [ref[g * TOK : (g + 1) * TOK, :] for ref in part_refs]
        attended = weighted([share[g : g + 1] for share in shares], outs, diagonal)
        attended_ref[:, g * HD : (g + 1) * HD] = attended.astype(BF16)


def merge(index, parts):
    return call_kernel(
        functools.partial(merge_kernel, len(parts)),
        index,
        list(parts),
        [jax.ShapeDtypeStruct((TOK, GROUP * HD), BF16), jax.ShapeDtypeStruct((GROUP, TOK), F32)],
        [],
        1_500_000_000,
    )


def ctx_pairs(dz, dh, dx):
    pairs = []
    for z in range(Z):
        for h in range(H):
            for x in range(X):
                to = ((z + dz) % Z) * H * X + ((h + dh) % H) * X + (x + dx) % X
                pairs.append((z * H * X + h * X + x, to))
    return pairs


def shift(value, dz=0, dh=0, dx=0):
    return lax.ppermute(value, "ctx", ctx_pairs(dz, dh, dx))


def flip_kvh(value, bit):
    return lax.ppermute(value, "kvh", [(i, i ^ bit) for i in range(4)])


def per_device(
    hidden,
    w_query,
    query_bias,
    w_key,
    key_bias,
    w_value,
    value_bias,
    prefix_keys,
    prefix_values,
    segment,
):
    kvh_index = lax.axis_index("kvh").astype(jnp.int32).reshape(1)
    ctx_index = lax.axis_index("ctx").astype(jnp.int32).reshape(1)
    segment = segment.reshape(1, TOK)

    barrier = lax.optimization_barrier
    far = flip_kvh(hidden, 2)
    near = flip_kvh(hidden, 1)

    own_unit = pack_prompt(prefix_keys[0], prefix_values[0])
    near, own_unit = barrier((near, own_unit))
    up1, down1 = shift(own_unit, dz=1), shift(own_unit, dz=-1)

    weights = (w_query, w_key, w_value)
    biases = (query_bias.reshape(1, ROWS), key_bias.reshape(1, HD), value_bias.reshape(1, HD))
    sums = project(kvh_index, (0, 1), (hidden, near), weights)
    far, sums, up1, down1 = barrier((far, sums, up1, down1))
    far_near = flip_kvh(far, 1)
    up2, down2 = shift(up1, dz=1), shift(down1, dz=-1)
    queries, block = project(kvh_index, (2, 3), (far, far_near), weights, sums, biases, segment)

    across = shift(queries, dh=1)
    row2, row3 = shift(queries, dx=2), shift(queries, dx=3)
    block8 = shift(block, dz=1)
    up2, row3 = barrier((up2, row3))
    up3 = shift(up2, dz=1)
    down2, row2 = barrier((down2, row2))
    down3 = shift(down2, dz=-1)
    row1 = shift(queries, dx=1)
    up3, block8 = barrier((up3, block8))
    up4 = shift(up3, dz=1)
    beyond1, beyond3 = shift(across, dx=1), shift(across, dx=3)
    beyond2 = shift(row2, dh=1)
    units = [own_unit, up1, down1, up2, down2, up3, down3, up4]
    blocks = [block, block8]

    def partials(*pairs):
        offsets, chosen = zip(*pairs)
        return prompt_partials(ctx_index, chosen, offsets, units, blocks)

    first = shift(partials(((1, 1), beyond1), ((1, 3), beyond3)), dh=1)
    second = shift(partials(((1, 2), beyond2), ((1, 0), across)), dh=1)
    mine = partials(((0, 1), row1), ((0, 3), row3), ((0, 2), row2))
    homeward = merge_pairs(ctx_index, mine, first, second)
    parts = [shift(part, dx=-dx) for dx, part in zip((1, 3, 2), homeward)]
    queries, homeward = barrier((queries, homeward))
    own = partials(((0, 0), queries))
    return tuple(merge(ctx_index, [own, second] + parts))


def solution(mesh):
    placed = (
        P("ctx", "kvh"),
        P(None, "kvh"),
        P("kvh"),
        P(None, "kvh"),
        P("kvh"),
        P(None, "kvh"),
        P("kvh"),
        P("kvh", "ctx", None),
        P("kvh", "ctx", None),
        P("ctx"),
    )
    return jax.shard_map(
        per_device,
        mesh=mesh,
        in_specs=placed,
        out_specs=(P("ctx", "kvh"), P("kvh", "ctx")),
        check_vma=False,
    )
```
